256 devices in a mesh: blk: 16 (over y_lo, z), panel: 16 (over x, y_hi, core).
Axes of the slice: x: 4, y: 4 (y_hi: 2, y_lo: 2; y = y_hi * 2 + y_lo), z: 8, core: 2. Of those that a mesh axis runs over, the one named last changes fastest.
Arguments:
- left_env: bfloat16 [16, 320, 16128], P('blk', 'panel'), may hold values from -6 to 6
- right_env: bfloat16 [16, 320, 16128], P('blk', 'panel'), may hold values from -6 to 6
- site_tensors: bfloat16 [16, 320, 2304], P('blk', 'panel'), may hold values from -0.625 to 0.625
- chain_operator: bfloat16 [28, 28, 4, 4], replicated, may hold values from -0.5 to 0.5
- targets: int32 [16, 320], P('blk', 'panel'), may hold values from 0 to 319, as said below
- sector_dims: int32 [320], replicated, may hold values from 12 to 24
Outputs:
- left_out: bfloat16 [16, 320, 16128], P('blk', 'panel')
- right_out: bfloat16 [16, 320, 16128], P('blk', 'panel')
The draws below stay inside these ranges and needn't reach their ends.
Inputs may be any that keep to these rules, and one draw needn't show every extreme that they name: `targets`: for each site, sector p * 20 + j has right sector ((p + c_j) mod 16) * 20 + pi_j, with offsets c_j and a permutation pi of 20 slots that depend on the site only; each row is a permutation of the 320 sectors; each offset is taken by at most 2 slots, and one offset by exactly 2.
All inputs are finite; a program needn't handle non-finite values.
Results may differ from the reference program's by a relative error of at most 0.0076.
Values may be sent and summed in bfloat16 or wider, within the bound.
No kernel may reach another device: no remote copies, remote signals or barrier semaphores. Data moves between devices by JAX's collectives and lax.ppermute only.
A program may use at most 64 MiB of HBM per device.

```python
import jax
import jax.numpy as jnp
from jax import lax

WD = 28
PHYS = 4
BLK = 24
SEC_DEV = 20
STEPS = 2
NSEC = 320
SITES = 16
CAP = 2


def draw_targets(key, part):
    key = jax.random.fold_in(key, 7)
    panels = NSEC // SEC_DEV

    def one_site(site_key):
        first_key, second_key, third_key = jax.random.split(site_key, 3)
        shuffled = jax.random.permutation(first_key, panels * CAP)
        busiest = jax.random.randint(second_key, (), 0, panels)
        others = (shuffled // CAP != busiest).astype(jnp.int32)
        ordering = jnp.argsort(others, stable=True)
        chosen = shuffled[ordering][:SEC_DEV]
        offsets = chosen // CAP
        landing = jax.random.permutation(third_key, SEC_DEV)
        owners = jnp.arange(panels)[:, None]
        mapped = (owners + offsets[None, :]) % panels * SEC_DEV + landing[None, :]
        return mapped.reshape(NSEC).astype(jnp.int32)
    return jax.vmap(one_site)(jax.random.split(key, SITES))


def touch_ends(result, stream_key, least, largest):
    longest = result.shape.index(max(result.shape))
    spots = []
    for shift in (0, 1):
        where = [jax.random.randint(jax.random.fold_in(stream_key, axis), (), 0, length) for axis, length in enumerate(result.shape)]
        where[longest] = (where[longest] + shift) % result.shape[longest]
        spots.append(tuple(where))
    return result.at[spots[0]].set(least).at[spots[1]].set(largest)


def level_of(key, extent, shards, low, high):
    gain = 1.0
    for position, blocks in shards:
        draws = jax.random.uniform(jax.random.fold_in(jax.random.fold_in(key, 6), position), (blocks,), jnp.float32, low / len(shards), high / len(shards))
        gain = gain * jnp.repeat(jnp.exp(draws), extent[position] // blocks).reshape((-1,) + (1,) * (len(extent) - 1 - position))
    return gain


def bell_draw(stream_key, extent, scale, limit, shards=(), dtype=jnp.bfloat16):
    drawn = scale * jax.random.normal(stream_key, extent, jnp.float32)
    if shards:
        drawn = drawn * level_of(stream_key, extent, shards, -0.22, 0.18)
    return jnp.clip(drawn, -limit, limit).astype(dtype)


def setup_inputs(seed: int = 0) -> dict:
    arg_keys = jax.random.split(jax.random.key(seed), 7)
    left_env = bell_draw(arg_keys[0], (SITES, NSEC, WD * BLK * BLK), 1.0, 6.0, ((0, 16), (1, 16)))
    right_env = bell_draw(arg_keys[1], (SITES, NSEC, WD * BLK * BLK), 1.0, 6.0, ((0, 16), (1, 16)))
    site_tensors = bell_draw(arg_keys[2], (SITES, NSEC, PHYS * BLK * BLK), (PHYS * BLK) ** -0.5, 0.625, ((0, 16), (1, 16)))
    chain_operator = bell_draw(arg_keys[3], (WD, WD, PHYS, PHYS), (WD * PHYS) ** -0.5, 0.5)
    targets = draw_targets(jax.random.fold_in(arg_keys[6], 71), 0)
    sector_dims = touch_ends(jax.random.randint(arg_keys[5], (NSEC,), BLK // 2, BLK + 1), jax.random.fold_in(arg_keys[5], 1), BLK // 2, BLK).astype(jnp.int32)
    return {"left_env": left_env, "right_env": right_env, "site_tensors": site_tensors, "chain_operator": chain_operator, "targets": targets, "sector_dims": sector_dims}


def masked(tensor, rows, cols):
    span = jnp.arange(BLK)
    keep_rows = (span[None, :] < rows[:, None])[:, None, :, None]
    keep_cols = (span[None, :] < cols[:, None])[:, None, None, :]
    keep = (keep_rows & keep_cols).astype(jnp.bfloat16)
    return tensor.reshape(-1, PHYS, BLK, BLK) * keep


def left_update(state, blocks, operator):
    count = state.shape[0]
    ket = state.reshape(count, WD, BLK, BLK).astype(jnp.float32)
    tensor = blocks.astype(jnp.float32)
    first = jnp.einsum('cwij,csjk->cwsik', ket, tensor).astype(jnp.bfloat16)
    second = jnp.einsum('wvts,cwsik->cvtik', operator.astype(jnp.float32), first.astype(jnp.float32)).astype(jnp.bfloat16)
    fresh = jnp.einsum('ctij,cvtik->cvjk', tensor, second.astype(jnp.float32)).astype(jnp.bfloat16)
    return fresh.reshape(count, -1)


def right_update(state, blocks, operator):
    count = state.shape[0]
    ket = state.reshape(count, WD, BLK, BLK).astype(jnp.float32)
    tensor = blocks.astype(jnp.float32)
    first = jnp.einsum('csij,cvjk->cvsik', tensor, ket).astype(jnp.bfloat16)
    second = jnp.einsum('wvts,cvsik->cwtik', operator.astype(jnp.float32), first.astype(jnp.float32)).astype(jnp.bfloat16)
    fresh = jnp.einsum('cwtik,ctjk->cwij', second.astype(jnp.float32), tensor).astype(jnp.bfloat16)
    return fresh.reshape(count, -1)


def reference(left_env, right_env, site_tensors, chain_operator, targets, sector_dims):
    def left_site(pieces):
        state, tensor, target = pieces
        blocks = masked(tensor, sector_dims, sector_dims[target])
        fresh = left_update(state, blocks, chain_operator)
        return jnp.zeros_like(fresh).at[target].set(fresh)

    def right_site(pieces):
        state, tensor, target = pieces
        blocks = masked(tensor, sector_dims, sector_dims[target])
        return right_update(state[target], blocks, chain_operator)

    left_now, right_now = left_env, right_env
    for turn_index in range(STEPS):
        left_now = jnp.roll(lax.map(left_site, (left_now, site_tensors, targets)), 1, axis=0)
        right_now = jnp.roll(lax.map(right_site, (right_now, site_tensors, targets)), -1, axis=0)
    return left_now, right_now
```

```python
import functools
import jax
import jax.numpy as jnp
from jax import lax
from jax.experimental import pallas as pl
from jax.experimental.pallas import tpu as pltpu
from jax.sharding import PartitionSpec as P

WD, PHYS, BLK = 28, 4, 24
WPAD = 32
SEC = 20
GRP = 5
LANES = 128
TILES = 144
ENV = WD * BLK * BLK
F32, BF16 = jnp.float32, jnp.bfloat16


def lane_ids(rows):
    return lax.broadcasted_iota(jnp.int32, (rows, LANES), 1)


def between(lane, low, high):
    return (lane >= low) & (lane < high)


def flat_to_rows(tiles, group, steps, rows):
    lane = lane_ids(steps)
    for b in range(16):
        acc = jnp.zeros((steps, LANES), F32)
        for c in range(GRP):
            first, last = 24 * b // LANES, (24 * b + 23) // LANES
            cut = 24 * c + (LANES * last - 24 * b if last > first else 24)
            for r in range(first, last + 1):
                piece = tiles[pl.ds((group * GRP + c) * 3 * steps + r, steps, stride=3), :]
                shift = (24 * c - 24 * b) % LANES
                if shift:
                    piece = pltpu.roll(piece, shift, 1)
                low, high = (24 * c, cut) if r == first else (cut, 24 * c + 24)
                acc = jnp.where(between(lane, low, high), piece, acc)
        rows[pl.ds(b, steps, stride=16), :] = acc


def rows_to_flat(rows, group, steps, tiles):
    lane = lane_ids(steps)
    for c in range(GRP):
        for r in range(3):
            acc = jnp.zeros((steps, LANES), F32)
            for b in range(16):
                low, high = max(24 * b - LANES * r, 0), min(24 * b + 24 - LANES * r, LANES)
                if low >= high:
                    continue
                piece = rows[pl.ds(b, steps, stride=16), :]
                shift = (24 * b - 24 * c) % LANES
                if shift:
                    piece = pltpu.roll(piece, shift, 1)
                acc = jnp.where(between(lane, low, high), piece, acc)
            tiles[pl.ds((group * GRP + c) * 3 * steps + r, steps, stride=3), :] = acc


def load_raw(raw, tiles, count):
    pad = tiles.shape[0] // SEC
    for n in range(count):
        tiles[pl.ds(n, SEC, stride=pad), :] = raw[:, n * LANES:(n + 1) * LANES].astype(F32)


def store_raw(tiles, raw, count):
    pad = tiles.shape[0] // SEC
    for n in range(count):
        raw[:, n * LANES:(n + 1) * LANES] = tiles[pl.ds(n, SEC, stride=pad), :].astype(BF16)


def load_wire(wire, tiles):
    for q in range(16):
        for m in range(SEC // 2):
            pair = wire[q, 16 * m:16 * m + 16, :].astype(F32)
            at = 2 * m * TILES + 8 * q
            tiles[at:at + 8, :] = pair[:8]
            tiles[at + TILES:at + TILES + 8, :] = pair[8:]


def store_wire(tiles, wire):
    for q in range(16):
        for m in range(SEC // 2):
            at = 2 * m * TILES + 8 * q
            pair = jnp.concatenate([tiles[at:at + 8, :], tiles[at + TILES:at + TILES + 8, :]], 0)
            wire[q, 16 * m:16 * m + 16, :] = pair.astype(BF16)


def site_rows(blocks, group, rows, spread):
    flat_to_rows(blocks, group, 8, rows)
    for s in range(PHYS):
        spread[pl.ds(s, BLK, stride=PHYS), :] = rows[s * BLK:(s + 1) * BLK, :]


def diagonal(rows, s):
    lane = lane_ids(BLK)
    block = rows[s * BLK:(s + 1) * BLK, :]
    parts = [jnp.where(between(lane, 24 * c, 24 * c + 24), block, 0.0) for c in range(GRP)]
    parts.append(jnp.zeros((8, LANES), F32))
    return jnp.concatenate(parts, 0)


def left_step(rows, rows_a, spread_a, operator, middle):
    diag = jnp.concatenate([diagonal(rows_a, s) for s in range(PHYS)], 1).astype(BF16)
    last = spread_a[...].T.astype(BF16)
    for p in range(6):
        env = jnp.concatenate([rows[pl.ds(4 * p + d, WPAD, stride=BLK), :] for d in range(4)], 0).astype(BF16)
        x = jnp.dot(env, diag, preferred_element_type=F32).astype(BF16)
        x = jnp.concatenate(
            [jnp.concatenate([x[:64, s * LANES:(s + 1) * LANES], x[64:, s * LANES:(s + 1) * LANES]], 1) for s in range(PHYS)], 0)
        y = jnp.dot(operator[...], x, preferred_element_type=F32)
        even = y[:, :LANES].reshape(WD, 8, LANES)
        odd = y[:, LANES:].reshape(WD, 8, LANES)
        middle[:, 16 * p:16 * p + 16, :] = jnp.concatenate([even, odd], 1).astype(BF16)
    lane = lane_ids(BLK)
    for u in range(WD // 2):
        y = jnp.concatenate([middle[2 * u], middle[2 * u + 1]], 1)
        out = jnp.dot(last, y, preferred_element_type=F32)
        for h in range(2):
            half = out[:, h * LANES:(h + 1) * LANES]
            acc = jnp.zeros((BLK, LANES), F32)
            for c in range(GRP):
                acc = jnp.where(between(lane, 24 * c, 24 * c + 24), half[24 * c:24 * c + 24], acc)
            rows[(2 * u + h) * BLK:(2 * u + h + 1) * BLK, :] = acc


def right_step(rows, rows_a, spread_a, operator, middle):
    first = spread_a[...].astype(BF16)
    diag = jnp.concatenate([diagonal(rows_a, s).T for s in range(PHYS)], 0).astype(BF16)
    lane = lane_ids(BLK)
    zeros = jnp.zeros((8, LANES), F32)
    for u in range(WD // 2):
        halves = []
        for h in range(2):
            block = rows[(2 * u + h) * BLK:(2 * u + h + 1) * BLK, :]
            parts = [jnp.where(between(lane, 24 * c, 24 * c + 24), block, 0.0) for c in range(GRP)]
            halves.append(jnp.concatenate(parts + [zeros], 0))
        z = jnp.dot(first, jnp.concatenate(halves, 1).astype(BF16), preferred_element_type=F32)
        even = z[:, :LANES].reshape(12, 8, LANES)
        odd = z[:, LANES:].reshape(12, 8, LANES)
        middle[:, 16 * u:16 * u + 16, :] = jnp.concatenate([even, odd], 1).astype(BF16)
    for p in range(6):
        z = jnp.concatenate([middle[2 * p], middle[2 * p + 1]], 1)
        v = jnp.dot(operator[...], z, preferred_element_type=F32).astype(BF16)
        v = jnp.concatenate(
            [jnp.concatenate([v[64 * t:64 * t + 64, h * LANES:(h + 1) * LANES] for t in range(PHYS)], 1) for h in range(2)], 0)
        out = jnp.dot(v, diag, preferred_element_type=F32)
        for d in range(4):
            rows[pl.ds(4 * p + d, WPAD, stride=BLK), :] = out[d * WPAD:(d + 1) * WPAD, :]


def env_kernel(steps, source, result, *refs):
    env, refs = refs[0], refs[1:]
    sites, refs = refs[:len(steps)], refs[len(steps):]
    operator, out, tiles, rows, rows_a, spread_a, middle = refs[:7]
    blocks = refs[7:]
    for c in range(SEC):
        tiles[c * TILES + 120:(c + 1) * TILES, :] = jnp.zeros((TILES - 120, LANES), F32)
    if source == "raw":
        load_raw(env, tiles, ENV // LANES)
    else:
        load_wire(env, tiles)
    for site, block in zip(sites, blocks):
        for c in range(SEC):
            block[c * 24 + 16:c * 24 + 24, :] = jnp.zeros((8, LANES), F32)
        load_raw(site, block, 18)

    def one(group, carry):
        flat_to_rows(tiles, group, 48, rows)
        for step, block in zip(steps, blocks):
            site_rows(block, group, rows_a, spread_a)
            (left_step if step == "L" else right_step)(rows, rows_a, spread_a, operator, middle)
        rows_to_flat(rows, group, 48, tiles)
        return carry

    lax.fori_loop(0, SEC // GRP, one, 0)
    if result == "raw":
        store_raw(tiles, out, ENV // LANES)
    else:
        store_wire(tiles, out)


def update(steps, source, result, env, sites, operator):
    shape = (SEC, ENV) if result == "raw" else (16, 160, LANES)
    middle = (WD, 96, LANES) if steps[0] == "L" else (12, 224, LANES)
    return pl.pallas_call(
        functools.partial(env_kernel, steps, source, result),
        out_shape=jax.ShapeDtypeStruct(shape, BF16),
        in_specs=[pl.BlockSpec(memory_space=pltpu.VMEM)] * (2 + len(sites)),
        out_specs=pl.BlockSpec(memory_space=pltpu.VMEM),
        scratch_shapes=[
            pltpu.VMEM((SEC * TILES, LANES), F32),
            pltpu.VMEM((WPAD * BLK, LANES), F32),
            pltpu.VMEM((LANES, LANES), F32),
            pltpu.VMEM((PHYS * BLK, LANES), F32),
            pltpu.VMEM(middle, BF16),
        ] + [pltpu.VMEM((SEC * 24, LANES), F32)] * len(sites),
        compiler_params=pltpu.CompilerParams(vmem_limit_bytes=40 * 1024 * 1024),
        cost_estimate=pl.CostEstimate(flops=2000000000 * len(sites), bytes_accessed=2000000, transcendentals=0),
        name="update_" + "".join(steps).lower(),
    )(env, *sites, operator)


def left_operator(op):
    same = jnp.eye(2, dtype=BF16)
    wide = jnp.pad(op, ((0, WPAD - WD), (0, 0), (0, 0), (0, 0)))
    return jnp.einsum("wvts,ab->vatsbw", wide, same).reshape(WD * 8, 8 * WPAD)


def right_operator(op):
    same = jnp.eye(2, dtype=BF16)
    wide = jnp.pad(op, ((0, WPAD - WD), (0, 0), (0, 0), (0, 0)))
    return jnp.einsum("wvts,ab->tawvbs", wide, same).reshape(8 * WPAD, WD * 8)


def permute_kernel(order, wire, out, held):
    for q in range(16):
        for m in range(SEC // 2):
            at = (q * SEC + 2 * m) * 8
            held[at:at + 16, :] = wire[q, 16 * m:16 * m + 16, :].astype(F32)
    for q in range(16):
        for m in range(SEC // 2):
            pair = [held[pl.ds(pl.multiple_of(order[q * SEC + 2 * m + h] * 8, 8), 8), :] for h in range(2)]
            out[q, 16 * m:16 * m + 16, :] = jnp.concatenate(pair, 0).astype(BF16)


def permute(order, wire):
    return pl.pallas_call(
        permute_kernel,
        out_shape=jax.ShapeDtypeStruct(wire.shape, BF16),
        in_specs=[pl.BlockSpec(memory_space=pltpu.SMEM), pl.BlockSpec(memory_space=pltpu.VMEM)],
        out_specs=pl.BlockSpec(memory_space=pltpu.VMEM),
        scratch_shapes=[pltpu.VMEM((16 * 160, LANES), F32)],
        compiler_params=pltpu.CompilerParams(vmem_limit_bytes=16 * 1024 * 1024),
        cost_estimate=pl.CostEstimate(flops=1000000, bytes_accessed=1400000, transcendentals=0),
        name="permute",
    )(order, wire)


def shifted(x, by):
    length = lax.axis_size("blk")
    return lax.ppermute(x, "blk", [(i, (i + by) % length) for i in range(length)])


def exchanged(x):
    return lax.all_to_all(x, "panel", split_axis=0, concat_axis=0, tiled=True)


def spread_and_collect(wire, order):
    return exchanged(permute(order, exchanged(wire)))


def pick(values, index):
    hits = index[:, None] == jnp.arange(values.shape[0])[None, :]
    return jnp.sum(jnp.where(hits, values[None, :], 0), axis=1)


def right_order(c0, s0, c1, s1):
    panels = jnp.arange(16)[:, None]
    offset, slot = c1 + pick(c0, s1), pick(s0, s1)
    return ((panels + offset[None, :]) % 16 * SEC + slot[None, :]).reshape(-1)


def left_order(c1, s1, c2, s2):
    panels = jnp.arange(16)[:, None]
    offset, slot = c2 + pick(c1, s2), pick(s1, s2)
    hits = jnp.arange(SEC)[:, None] == slot[None, :]
    source = jnp.sum(jnp.where(hits, jnp.arange(SEC)[None, :], 0), axis=1)
    back = jnp.sum(jnp.where(hits, offset[None, :], 0), axis=1)
    return ((panels - back[None, :]) % 16 * SEC + source[None, :]).reshape(-1)


def fetch_sites(blocks, me, c1, s1):
    slots = jnp.arange(SEC)
    rank = jnp.sum((c1[None, :] == c1[:, None]) & (slots[None, :] < slots[:, None]), axis=1)
    place = jnp.arange(32)
    wanted = ((me - place // 2) % 16)[:, None] == c1[None, :]
    wanted = wanted & ((place % 2)[:, None] == rank[None, :])
    send = jnp.sum(jnp.where(wanted[:, :, None] & (s1[:, None] == slots[None, :])[None], 1.0, 0.0), axis=1)
    packed = jnp.dot(send.astype(BF16), blocks, preferred_element_type=F32).astype(BF16)
    arrived = exchanged(packed.reshape(16, 2, -1)).reshape(32, -1)
    take = ((me + c1) % 16 * 2 + rank)[:, None] == place[None, :]
    return jnp.dot(take.astype(BF16), arrived, preferred_element_type=F32).astype(BF16)


def masked(tensor, rows, cols):
    place = jnp.arange(tensor.shape[1])
    keep = ((place // BLK % BLK)[None, :] < rows[:, None]) & ((place % BLK)[None, :] < cols[:, None])
    return jnp.where(keep, tensor, jnp.zeros((), BF16))


def body(left_env, right_env, site_tensors, chain_operator, targets, sector_dims):
    me = lax.axis_index("panel")
    target = targets[0]
    rows = lax.dynamic_slice_in_dim(sector_dims, me * SEC, SEC)
    blocks = masked(site_tensors[0], rows, pick(sector_dims, target))
    code = (target // SEC - me) % 16 * SEC + target % SEC
    code1, code2 = shifted(code, 1), shifted(code, 2)
    c0, s0, c1, s1, c2, s2 = code // SEC, code % SEC, code1 // SEC, code1 % SEC, code2 // SEC, code2 % SEC
    blocks1 = shifted(blocks, 1)

    wire = jnp.pad(right_env[0], ((0, 0), (0, 256))).reshape(SEC, 16, 8, LANES)
    wire = wire.transpose(1, 0, 2, 3).reshape(16, 160, LANES)
    arrived = spread_and_collect(wire, right_order(c0, s0, c1, s1))
    fetched = fetch_sites(blocks, me, c1, s1)
    right = update(("R", "R"), "wire", "raw", arrived, [fetched, blocks1], right_operator(chain_operator))
    right_out = shifted(right, -2)

    operator = left_operator(chain_operator)
    left = update(("L",), "raw", "wire", left_env[0], [blocks], operator)
    left = shifted(left, 2)
    left = update(("L",), "wire", "wire", left, [shifted(fetched, 1)], operator)
    left = spread_and_collect(left, left_order(c1, s1, c2, s2))
    left_out = left.reshape(16, SEC, 8, LANES).transpose(1, 0, 2, 3).reshape(SEC, -1)[:, :ENV]
    return left_out[None], right_out[None]


def solution(mesh):
    whole = P("blk", "panel", None)
    return jax.shard_map(
        body,
        mesh=mesh,
        in_specs=(whole, whole, whole, P(), P("blk", "panel"), P()),
        out_specs=(whole, whole),
        check_vma=False,
    )
```

```python
import functools
import jax
import jax.numpy as jnp
from jax import lax
from jax.experimental import pallas as pl
from jax.experimental.pallas import tpu as pltpu
from jax.sharding import PartitionSpec as P

WD, PHYS, BLK = 28, 4, 24
WPAD = 32
SEC = 20
FIRST, SECOND, WHOLE = (0, 2), (2, 2), (0, 4)
GRP = 5
LANES = 128
TILES = 144
ENV = WD * BLK * BLK
F32, BF16 = jnp.float32, jnp.bfloat16


def lane_ids(rows):
    return lax.broadcasted_iota(jnp.int32, (rows, LANES), 1)


def between(lane, low, high):
    return (lane >= low) & (lane < high)


def spans(b):
    out = []
    for r in range(3):
        low, high = max(24 * b - LANES * r, 0), min(24 * b + 24 - LANES * r, LANES)
        if low < high:
            out.append((r, low, high))
    return out


def merge(lane, pieces):
    acc = None
    for value, low, high in pieces:
        acc = value if acc is None else jnp.where(between(lane, low, high), value, acc)
    return acc


def turned(value, shift):
    return pltpu.roll(value, shift % LANES, 1) if shift % LANES else value


def flat_to_rows(tiles, group, steps, rows):
    lane = lane_ids(steps)
    live = lane < GRP * BLK
    shifted_by = {}

    def source(c, r):
        return tiles[pl.ds((group * GRP + c) * 3 * steps + r, steps, stride=3), :]

    for b in range(16):
        for d in range(-b, GRP - b):
            if d not in shifted_by:
                pieces = [(source(c, r), low, high) for c in range(GRP) if 0 <= c - d < 16 for r, low, high in spans(c - d)]
                shifted_by[d] = turned(merge(lane, pieces), 24 * d)
        acc = merge(lane, [(shifted_by[c - b], 24 * c, 24 * c + 24) for c in range(GRP)])
        rows[pl.ds(b, steps, stride=16), :] = jnp.where(live, acc, 0.0)
        del shifted_by[GRP - 1 - b]


def rows_to_flat(rows, group, steps, tiles):
    lane = lane_ids(steps)
    for r in range(3):
        shifted_by = {}
        inside = [(b, low, high) for b in range(16) for tile, low, high in spans(b) if tile == r]
        for c in range(GRP):
            pieces = []
            for b, low, high in inside:
                d = c - b
                if d not in shifted_by:
                    parts = [(rows[pl.ds(e - d, steps, stride=16), :], 24 * e, 24 * e + 24) for e in range(GRP) if 0 <= e - d < 16]
                    shifted_by[d] = turned(merge(lane, parts), -24 * d)
                pieces.append((shifted_by[d], low, high))
            tiles[pl.ds((group * GRP + c) * 3 * steps + r, steps, stride=3), :] = merge(lane, pieces)


def load_raw(raw, tiles, count):
    pad = tiles.shape[0] // SEC
    for n in range(count):
        tiles[pl.ds(n, SEC, stride=pad), :] = raw[:, n * LANES:(n + 1) * LANES].astype(F32)


def store_raw(tiles, raw, count):
    pad = tiles.shape[0] // SEC
    for n in range(count):
        raw[:, n * LANES:(n + 1) * LANES] = tiles[pl.ds(n, SEC, stride=pad), :].astype(BF16)


def load_wire(wire, tiles):
    for q in range(16):
        for m in range(SEC // 2):
            pair = wire[q, 16 * m:16 * m + 16, :].astype(F32)
            at = 2 * m * TILES + 8 * q
            tiles[at:at + 8, :] = pair[:8]
            tiles[at + TILES:at + TILES + 8, :] = pair[8:]


def store_wire(tiles, wire):
    for q in range(16):
        for m in range(SEC // 2):
            at = 2 * m * TILES + 8 * q
            pair = jnp.concatenate([tiles[at:at + 8, :], tiles[at + TILES:at + TILES + 8, :]], 0)
            wire[q, 16 * m:16 * m + 16, :] = pair.astype(BF16)


def site_rows(blocks, group, rows, spread):
    flat_to_rows(blocks, group, 8, rows)
    for s in range(PHYS):
        spread[pl.ds(s, BLK, stride=PHYS), :] = rows[s * BLK:(s + 1) * BLK, :]


def diagonal(rows, s):
    lane = lane_ids(BLK)
    block = rows[s * BLK:(s + 1) * BLK, :]
    parts = [jnp.where(between(lane, 24 * c, 24 * c + 24), block, 0.0) for c in range(GRP)]
    parts.append(jnp.zeros((8, LANES), F32))
    return jnp.concatenate(parts, 0)


def left_step(rows, rows_a, spread_a, operator, middle):
    diag = jnp.concatenate([diagonal(rows_a, s) for s in range(PHYS)], 1).astype(BF16)
    last = spread_a[...].T.astype(BF16)
    for p in range(6):
        env = jnp.concatenate([rows[pl.ds(4 * p + d, WPAD, stride=BLK), :] for d in range(4)], 0).astype(BF16)
        x = jnp.dot(env, diag, preferred_element_type=F32).astype(BF16)
        x = jnp.concatenate(
            [jnp.concatenate([x[:64, s * LANES:(s + 1) * LANES], x[64:, s * LANES:(s + 1) * LANES]], 1) for s in range(PHYS)], 0)
        y = jnp.dot(operator[...], x, preferred_element_type=F32)
        even = y[:, :LANES].reshape(WD, 8, LANES)
        odd = y[:, LANES:].reshape(WD, 8, LANES)
        middle[:, 16 * p:16 * p + 16, :] = jnp.concatenate([even, odd], 1).astype(BF16)
    lane = lane_ids(BLK)
    for u in range(WD // 2):
        y = jnp.concatenate([middle[2 * u], middle[2 * u + 1]], 1)
        out = jnp.dot(last, y, preferred_element_type=F32)
        for h in range(2):
            half = out[:, h * LANES:(h + 1) * LANES]
            acc = jnp.zeros((BLK, LANES), F32)
            for c in range(GRP):
                acc = jnp.where(between(lane, 24 * c, 24 * c + 24), half[24 * c:24 * c + 24], acc)
            rows[(2 * u + h) * BLK:(2 * u + h + 1) * BLK, :] = acc


def right_step(rows, rows_a, spread_a, operator, middle):
    first = spread_a[...].astype(BF16)
    diag = jnp.concatenate([diagonal(rows_a, s).T for s in range(PHYS)], 0).astype(BF16)
    lane = lane_ids(BLK)
    zeros = jnp.zeros((8, LANES), F32)
    for u in range(WD // 2):
        halves = []
        for h in range(2):
            block = rows[(2 * u + h) * BLK:(2 * u + h + 1) * BLK, :]
            parts = [jnp.where(between(lane, 24 * c, 24 * c + 24), block, 0.0) for c in range(GRP)]
            halves.append(jnp.concatenate(parts + [zeros], 0))
        z = jnp.dot(first, jnp.concatenate(halves, 1).astype(BF16), preferred_element_type=F32)
        even = z[:, :LANES].reshape(12, 8, LANES)
        odd = z[:, LANES:].reshape(12, 8, LANES)
        middle[:, 16 * u:16 * u + 16, :] = jnp.concatenate([even, odd], 1).astype(BF16)
    for p in range(6):
        z = jnp.concatenate([middle[2 * p], middle[2 * p + 1]], 1)
        v = jnp.dot(operator[...], z, preferred_element_type=F32).astype(BF16)
        v = jnp.concatenate(
            [jnp.concatenate([v[64 * t:64 * t + 64, h * LANES:(h + 1) * LANES] for t in range(PHYS)], 1) for h in range(2)], 0)
        out = jnp.dot(v, diag, preferred_element_type=F32)
        for d in range(4):
            rows[pl.ds(4 * p + d, WPAD, stride=BLK), :] = out[d * WPAD:(d + 1) * WPAD, :]


def load_sites(site, block):
    if site.shape[0] == SEC:
        for c in range(SEC):
            block[c * 24 + 16:c * 24 + 24, :] = jnp.zeros((8, LANES), F32)
        load_raw(site, block, 18)
    else:
        block[...] = site[...].astype(F32)


def clear_tails(tiles):
    for c in range(SEC):
        tiles[c * TILES + 120:(c + 1) * TILES, :] = jnp.zeros((TILES - 120, LANES), F32)


def load_part(part, tiles, groups):
    for m in range(GRP * groups[1]):
        at = (GRP * groups[0] + m) * TILES
        tiles[at:at + LANES, :] = part[m].astype(F32)


def store_part(tiles, part, groups):
    for m in range(GRP * groups[1]):
        at = (GRP * groups[0] + m) * TILES
        part[m] = tiles[at:at + LANES, :].astype(BF16)


def update_kernel(steps, source, result, groups, count, *refs):
    env, sites, operator = refs[0], refs[1:1 + len(steps)], refs[1 + len(steps)]
    refs = refs[count:]
    out, tiles, rows, rows_a, spread_a, middle = refs[:6]
    blocks = refs[6:]
    if source != "rows":
        clear_tails(tiles)
        (load_raw if source == "raw" else load_wire)(env, tiles, *([ENV // LANES] if source == "raw" else []))
    else:
        rows[WD * BLK:, :] = jnp.zeros(((WPAD - WD) * BLK, LANES), F32)
    for site, block in zip(sites, blocks):
        load_sites(site, block)

    def one(local, carry):
        group = local + groups[0]
        if source == "rows":
            rows[:WD * BLK, :] = env[local].astype(F32)
        else:
            flat_to_rows(tiles, group, 48, rows)
        for step, block in zip(steps, blocks):
            site_rows(block, group, rows_a, spread_a)
            (left_step if step == "L" else right_step)(rows, rows_a, spread_a, operator, middle)
        if result == "rows":
            out[local] = rows[:WD * BLK, :].astype(BF16)
        else:
            rows_to_flat(rows, group, 48, tiles)
        return carry

    lax.fori_loop(0, groups[1], one, 0)
    if result == "part":
        store_part(tiles, out, groups)
    elif result == "raw":
        store_raw(tiles, out, ENV // LANES)
    elif result == "wire":
        store_wire(tiles, out)


def update(steps, source, result, groups, env, sites, operator, *tickets):
    shape = {"rows": (groups[1], WD * BLK, LANES), "part": (GRP * groups[1], LANES, LANES), "wire": (16, 160, LANES), "raw": (SEC, ENV)}[result]
    middle = (WD, 96, LANES) if steps[0] == "L" else (12, 224, LANES)
    inputs = [env, *sites, operator, *tickets]
    return pl.pallas_call(
        functools.partial(update_kernel, steps, source, result, groups, len(inputs)),
        out_shape=jax.ShapeDtypeStruct(shape, BF16),
        in_specs=[pl.BlockSpec(memory_space=pltpu.VMEM)] * (2 + len(sites)) + [pl.BlockSpec(memory_space=pl.ANY)] * len(tickets),
        out_specs=pl.BlockSpec(memory_space=pltpu.VMEM),
        scratch_shapes=[
            pltpu.VMEM((SEC * TILES, LANES), F32),
            pltpu.VMEM((WPAD * BLK, LANES), F32),
            pltpu.VMEM((LANES, LANES), F32),
            pltpu.VMEM((PHYS * BLK, LANES), F32),
            pltpu.VMEM(middle, BF16),
        ] + [pltpu.VMEM((SEC * 24, LANES), F32)] * len(sites),
        compiler_params=pltpu.CompilerParams(vmem_limit_bytes=32 * 1024 * 1024),
        cost_estimate=pl.CostEstimate(flops=(2300000000 if steps[0] == "L" else 600000000) * groups[1] * len(sites), bytes_accessed=100000, transcendentals=0),
        name="update_" + "".join(steps).lower() + str(groups[0]),
    )(*inputs)


def left_operator(op):
    same = jnp.eye(2, dtype=BF16)
    wide = jnp.pad(op, ((0, WPAD - WD), (0, 0), (0, 0), (0, 0)))
    return jnp.einsum("wvts,ab->vatsbw", wide, same).reshape(WD * 8, 8 * WPAD)


def right_operator(op):
    same = jnp.eye(2, dtype=BF16)
    wide = jnp.pad(op, ((0, WPAD - WD), (0, 0), (0, 0), (0, 0)))
    return jnp.einsum("wvts,ab->tawvbs", wide, same).reshape(8 * WPAD, WD * 8)


def call(kernel, name, shapes, inputs, scratch, in_smem=0):
    spaces = [pltpu.SMEM] * in_smem + [pltpu.VMEM] * (len(inputs) - in_smem)
    return pl.pallas_call(
        kernel,
        out_shape=[jax.ShapeDtypeStruct(shape, BF16) for shape in shapes],
        in_specs=[pl.BlockSpec(memory_space=space) for space in spaces],
        out_specs=[pl.BlockSpec(memory_space=pltpu.VMEM)] * len(shapes),
        scratch_shapes=scratch,
        compiler_params=pltpu.CompilerParams(vmem_limit_bytes=32 * 1024 * 1024),
        cost_estimate=pl.CostEstimate(flops=2000000000, bytes_accessed=100000, transcendentals=0),
        name=name,
    )(*inputs)


def wire_kernel(raw, out, tiles):
    clear_tails(tiles)
    load_raw(raw, tiles, ENV // LANES)
    store_wire(tiles, out)


def to_wire(raw):
    return call(wire_kernel, "to_wire", [(16, 160, LANES)], [raw], [pltpu.VMEM((SEC * TILES, LANES), F32)])[0]


def permute_wire(order, wire, out, held):
    for q in range(16):
        for m in range(SEC // 2):
            at = (q * SEC + 2 * m) * 8
            held[at:at + 16, :] = wire[q, 16 * m:16 * m + 16, :].astype(F32)
    for q in range(16):
        for m in range(SEC // 2):
            pair = [held[pl.ds(pl.multiple_of(order[q * SEC + 2 * m + h] * 8, 8), 8), :] for h in range(2)]
            out[q, 16 * m:16 * m + 16, :] = jnp.concatenate(pair, 0).astype(BF16)


def permute_pack_kernel(order, chosen, wire, sites, sites1, out, held, block, block1):
    permute_wire(order, wire, out, held)
    load_sites(sites, block)
    load_sites(sites1, block1)
    for q in range(16):
        for n, source in enumerate((block, block1)):
            pair = [source[pl.ds(pl.multiple_of(chosen[32 * n + 2 * q + h] * 24, 8), 24), :] for h in range(2)]
            out[q, 160 + 48 * n:208 + 48 * n, :] = jnp.concatenate(pair, 0).astype(BF16)


def permute_pack(order, chosen, wire, sites, sites1):
    scratch = [pltpu.VMEM((16 * 160, LANES), F32)] + [pltpu.VMEM((SEC * 24, LANES), F32)] * 2
    return call(permute_pack_kernel, "permute_pack", [(16, 256, LANES)], [order, chosen, wire, sites, sites1], scratch, 2)[0]


def fetch_kernel(places, wire, fetched, pushed, extra):
    for q in range(16):
        extra[q * 96:q * 96 + 96, :] = wire[q, 160:256, :].astype(F32)
    for n, out in enumerate((fetched, pushed)):
        for m in range(SEC // 2):
            pair = [extra[pl.ds(pl.multiple_of(places[SEC * n + 2 * m + h] * 24, 8), 24), :] for h in range(2)]
            out[48 * m:48 * m + 48, :] = jnp.concatenate(pair, 0).astype(BF16)


def fetch(places, wire):
    return call(fetch_kernel, "fetch", [(SEC * 24, LANES)] * 2, [places, wire], [pltpu.VMEM((16 * 96, LANES), F32)], 1)


def touch_kernel(value, out):
    out[...] = jnp.zeros((16, LANES), BF16)


def touch(value):
    return pl.pallas_call(
        touch_kernel,
        out_shape=jax.ShapeDtypeStruct((16, LANES), BF16),
        in_specs=[pl.BlockSpec(memory_space=pl.ANY)],
        out_specs=pl.BlockSpec(memory_space=pltpu.VMEM),
        cost_estimate=pl.CostEstimate(flops=20000000000, bytes_accessed=1000, transcendentals=0),
        name="touch",
    )(value)


def permute(order, wire):
    return call(permute_wire, "permute", [(16, 160, LANES)], [order, wire], [pltpu.VMEM((16 * 160, LANES), F32)], 1)[0]


def join_kernel(first, second, out, tiles):
    load_part(first, tiles, FIRST)
    load_part(second, tiles, SECOND)
    store_raw(tiles, out, ENV // LANES)


def join(first, second):
    return call(join_kernel, "join", [(SEC, ENV)], [first, second], [pltpu.VMEM((SEC * TILES, LANES), F32)])[0]


def shifted(x, by):
    length = lax.axis_size("blk")
    return lax.ppermute(x, "blk", [(i, (i + by) % length) for i in range(length)])


def exchanged(x):
    return lax.all_to_all(x, "panel", split_axis=0, concat_axis=0, tiled=True)


def after(x, *others):
    return lax.optimization_barrier((x, *others))[0]


def pick(values, index):
    hits = index[:, None] == jnp.arange(values.shape[0])[None, :]
    return jnp.sum(jnp.where(hits, values[None, :], 0), axis=1)


def right_order(c0, s0, c1, s1):
    panels = jnp.arange(16)[:, None]
    offset, slot = c1 + pick(c0, s1), pick(s0, s1)
    return ((panels + offset[None, :]) % 16 * SEC + slot[None, :]).reshape(-1)


def left_order(c1, s1, c2, s2):
    panels = jnp.arange(16)[:, None]
    offset, slot = c2 + pick(c1, s2), pick(s1, s2)
    hits = jnp.arange(SEC)[:, None] == slot[None, :]
    source = jnp.sum(jnp.where(hits, jnp.arange(SEC)[None, :], 0), axis=1)
    back = jnp.sum(jnp.where(hits, offset[None, :], 0), axis=1)
    return ((panels - back[None, :]) % 16 * SEC + source[None, :]).reshape(-1)


def move_plan(me, c1, s1):
    slots = jnp.arange(SEC)
    rank = jnp.sum((c1[None, :] == c1[:, None]) & (slots[None, :] < slots[:, None]), axis=1)
    place = jnp.arange(32)
    same = (place % 2)[:, None] == rank[None, :]
    asked = same & (((me - place // 2) % 16)[:, None] == c1[None, :])
    pushed = same & (((place // 2 - me) % 16)[:, None] == c1[None, :])
    chosen = [jnp.sum(jnp.where(asked, s1[None, :], 0), axis=1), jnp.sum(jnp.where(pushed, slots[None, :], 0), axis=1)]
    landing = slots[:, None] == s1[None, :]
    back = jnp.sum(jnp.where(landing, ((me - c1) % 16 * 4 + 2 + rank)[None, :], 0), axis=1)
    return jnp.concatenate(chosen), jnp.concatenate([(me + c1) % 16 * 4 + rank, back])


def masked(tensor, rows, cols):
    place = jnp.arange(tensor.shape[1])
    keep = ((place // BLK % BLK)[None, :] < rows[:, None]) & ((place % BLK)[None, :] < cols[:, None])
    return jnp.where(keep, tensor, jnp.zeros((), BF16))


def body(left_env, right_env, site_tensors, chain_operator, targets, sector_dims):
    me = lax.axis_index("panel")
    wire = to_wire(right_env[0])
    arrived = exchanged(wire)

    target = after(targets[0], wire)
    code = (target // SEC - me) % 16 * SEC + target % SEC
    rows = lax.dynamic_slice_in_dim(sector_dims, me * SEC, SEC)
    blocks = masked(site_tensors[0], rows, pick(sector_dims, target))
    operator = left_operator(after(chain_operator, wire))
    left = update(("L",), "raw", "wire", WHOLE, left_env[0], [blocks], operator)
    left_moved = shifted(left, 2)
    code1, blocks1 = shifted(code, 1), shifted(blocks, 1)
    code2 = shifted(after(code, left), 2)

    c0, s0, c1, s1 = code // SEC, code % SEC, code1 // SEC, code1 % SEC
    chosen, places = move_plan(me, c1, s1)
    wire = permute_pack(right_order(c0, s0, c1, s1), chosen, after(arrived, left), blocks, blocks1)
    right = exchanged(wire)
    fetched, pushed = fetch(places, right)

    operator_r = right_operator(after(chain_operator, wire))
    left = exchanged(after(left_moved, fetched))
    right0 = update(("R", "R"), "wire", "part", FIRST, right, [fetched, blocks1], operator_r, touch(left_moved))
    right0_moved = shifted(right0, -2)
    right1 = update(("R", "R"), "wire", "part", SECOND, after(right, right0), [fetched, blocks1], operator_r)
    right1_moved = shifted(right1, -2)
    code2 = after(code2, right0)
    c2, s2 = code2 // SEC, code2 % SEC
    left = exchanged(permute(left_order(c1, s1, c2, s2), after(left, right1)))
    left_out = update(("L",), "wire", "raw", WHOLE, left, [pushed], operator, touch(right0_moved))
    right_out = join(after(right0_moved, left_out), right1_moved)
    return left_out[None], right_out[None]


def solution(mesh):
    whole = P("blk", "panel", None)
    return jax.shard_map(
        body,
        mesh=mesh,
        in_specs=(whole, whole, whole, P(), P("blk", "panel"), P()),
        out_specs=(whole, whole),
        check_vma=False,
    )
```

```python
import functools
import jax
import jax.numpy as jnp
from jax import lax
from jax.experimental import pallas as pl
from jax.experimental.pallas import tpu as pltpu
from jax.sharding import PartitionSpec as P

WD, PHYS, BLK = 28, 4, 24
WPAD = 32
SEC = 20
FIRST, SECOND, WHOLE = (0, 2), (2, 2), (0, 4)
GRP = 5
LANES = 128
TILES = 144
ENV = WD * BLK * BLK
SITE = PHYS * BLK * BLK
F32, BF16 = jnp.float32, jnp.bfloat16


def lane_ids(rows):
    return lax.broadcasted_iota(jnp.int32, (rows, LANES), 1)


def between(lane, low, high):
    return (lane >= low) & (lane < high)


def spans(b):
    out = []
    for r in range(3):
        low, high = max(24 * b - LANES * r, 0), min(24 * b + 24 - LANES * r, LANES)
        if low < high:
            out.append((r, low, high))
    return out


def merge(lane, pieces):
    acc = None
    for value, low, high in pieces:
        acc = value if acc is None else jnp.where(between(lane, low, high), value, acc)
    return acc


def turned(value, shift):
    return pltpu.roll(value, shift % LANES, 1) if shift % LANES else value


def flat_to_rows(tiles, group, steps, rows):
    lane = lane_ids(steps)
    live = lane < GRP * BLK
    shifted_by = {}

    def source(c, r):
        return tiles[pl.ds((group * GRP + c) * 3 * steps + r, steps, stride=3), :]

    for b in range(16):
        for d in range(-b, GRP - b):
            if d not in shifted_by:
                pieces = [(source(c, r), low, high) for c in range(GRP) if 0 <= c - d < 16 for r, low, high in spans(c - d)]
                shifted_by[d] = turned(merge(lane, pieces), 24 * d)
        acc = merge(lane, [(shifted_by[c - b], 24 * c, 24 * c + 24) for c in range(GRP)])
        rows[pl.ds(b, steps, stride=16), :] = jnp.where(live, acc, 0.0)
        del shifted_by[GRP - 1 - b]


def rows_to_flat(rows, group, steps, tiles):
    lane = lane_ids(steps)
    for r in range(3):
        shifted_by = {}
        inside = [(b, low, high) for b in range(16) for tile, low, high in spans(b) if tile == r]
        for c in range(GRP):
            pieces = []
            for b, low, high in inside:
                d = c - b
                if d not in shifted_by:
                    parts = [(rows[pl.ds(e - d, steps, stride=16), :], 24 * e, 24 * e + 24) for e in range(GRP) if 0 <= e - d < 16]
                    shifted_by[d] = turned(merge(lane, parts), -24 * d)
                pieces.append((shifted_by[d], low, high))
            tiles[pl.ds((group * GRP + c) * 3 * steps + r, steps, stride=3), :] = merge(lane, pieces)


def load_raw(raw, tiles, count):
    pad = tiles.shape[0] // SEC
    for n in range(count):
        tiles[pl.ds(n, SEC, stride=pad), :] = raw[:, n * LANES:(n + 1) * LANES].astype(F32)


def store_raw(tiles, raw, count):
    pad = tiles.shape[0] // SEC
    for n in range(count):
        raw[:, n * LANES:(n + 1) * LANES] = tiles[pl.ds(n, SEC, stride=pad), :].astype(BF16)


def load_wire(wire, tiles):
    for q in range(16):
        for m in range(SEC // 2):
            pair = wire[q, 16 * m:16 * m + 16, :].astype(F32)
            at = 2 * m * TILES + 8 * q
            tiles[at:at + 8, :] = pair[:8]
            tiles[at + TILES:at + TILES + 8, :] = pair[8:]


def store_wire(tiles, wire):
    for q in range(16):
        for m in range(SEC // 2):
            at = 2 * m * TILES + 8 * q
            pair = jnp.concatenate([tiles[at:at + 8, :], tiles[at + TILES:at + TILES + 8, :]], 0)
            wire[q, 16 * m:16 * m + 16, :] = pair.astype(BF16)


def site_rows(blocks, group, rows, spread):
    flat_to_rows(blocks, group, 8, rows)
    for s in range(PHYS):
        spread[pl.ds(s, BLK, stride=PHYS), :] = rows[s * BLK:(s + 1) * BLK, :]


def diagonal(rows, s):
    lane = lane_ids(BLK)
    block = rows[s * BLK:(s + 1) * BLK, :]
    parts = [jnp.where(between(lane, 24 * c, 24 * c + 24), block, 0.0) for c in range(GRP)]
    parts.append(jnp.zeros((8, LANES), F32))
    return jnp.concatenate(parts, 0)


def widen(operator, wide, held):
    held[...] = jnp.zeros((2 * WD * 8, LANES), F32)
    for t in range(PHYS):
        value = operator[pl.ds(t, WD, stride=PHYS), :]
        for i in range(2):
            held[pl.ds(WD * 8 * i + PHYS * i + t, WD, stride=8), :] = value
    wide[...] = jnp.concatenate([held[:WD * 8, :], held[WD * 8:, :]], 1).astype(BF16)


def left_step(rows, rows_a, spread_a, operator, middle, spread):
    diag = jnp.concatenate([diagonal(rows_a, s) for s in range(PHYS)], 1).astype(BF16)
    last = spread_a[...].T.astype(BF16)
    env = jnp.concatenate([rows[pl.ds(d, WPAD, stride=BLK), :] for d in range(BLK)], 0).astype(BF16)
    xs = jnp.dot(env, diag, preferred_element_type=F32).astype(BF16)
    for p in range(6):
        x = xs[128 * p:128 * p + 128]
        for n in range(2):
            for s in range(PHYS):
                at = (4 * n + s) * WPAD
                spread[p, at:at + WPAD, :LANES] = x[n * WPAD:(n + 1) * WPAD, s * LANES:(s + 1) * LANES]
                spread[p, at:at + WPAD, LANES:] = x[64 + n * WPAD:64 + (n + 1) * WPAD, s * LANES:(s + 1) * LANES]
    for p in range(6):
        y = jnp.dot(operator[...], spread[p], preferred_element_type=F32)
        even = y[:, :LANES].reshape(WD, 8, LANES)
        odd = y[:, LANES:].reshape(WD, 8, LANES)
        middle[:, 16 * p:16 * p + 16, :] = jnp.concatenate([even, odd], 1).astype(BF16)
    lane = lane_ids(BLK)
    for u in range(WD // 2):
        y = jnp.concatenate([middle[2 * u], middle[2 * u + 1]], 1)
        out = jnp.dot(last, y, preferred_element_type=F32)
        for h in range(2):
            half = out[:, h * LANES:(h + 1) * LANES]
            acc = jnp.zeros((BLK, LANES), F32)
            for c in range(GRP):
                acc = jnp.where(between(lane, 24 * c, 24 * c + 24), half[24 * c:24 * c + 24], acc)
            rows[(2 * u + h) * BLK:(2 * u + h + 1) * BLK, :] = acc


def right_step(rows, rows_a, spread_a, operator, middle, spread):
    first = spread_a[...].astype(BF16)
    diag = jnp.concatenate([diagonal(rows_a, s).T for s in range(PHYS)], 0).astype(BF16)
    lane = lane_ids(BLK)
    zeros = jnp.zeros((8, LANES), F32)
    for u in range(WD // 2):
        halves = []
        for h in range(2):
            block = rows[(2 * u + h) * BLK:(2 * u + h + 1) * BLK, :]
            parts = [jnp.where(between(lane, 24 * c, 24 * c + 24), block, 0.0) for c in range(GRP)]
            halves.append(jnp.concatenate(parts + [zeros], 0))
        z = jnp.dot(first, jnp.concatenate(halves, 1).astype(BF16), preferred_element_type=F32)
        even = z[:, :LANES].reshape(12, 8, LANES)
        odd = z[:, LANES:].reshape(12, 8, LANES)
        middle[:, 16 * u:16 * u + 16, :] = jnp.concatenate([even, odd], 1).astype(BF16)
    for p in range(6):
        z = jnp.concatenate([middle[2 * p], middle[2 * p + 1]], 1)
        v = jnp.dot(operator[...], z, preferred_element_type=F32).astype(BF16)
        for h in range(2):
            for t in range(PHYS):
                spread[LANES * p + 64 * h:LANES * p + 64 * h + 64, t * LANES:(t + 1) * LANES] = v[64 * t:64 * t + 64, h * LANES:(h + 1) * LANES]
    out = jnp.dot(spread[...], diag, preferred_element_type=F32)
    for d in range(BLK):
        rows[pl.ds(d, WPAD, stride=BLK), :] = out[d * WPAD:(d + 1) * WPAD, :]


def load_sites(site, block):
    if site.shape[0] == SEC:
        for c in range(SEC):
            block[c * 24 + 16:c * 24 + 24, :] = jnp.zeros((8, LANES), F32)
        load_raw(site, block, 18)
    else:
        block[...] = site[...].astype(F32)


def clear_tails(tiles):
    for c in range(SEC):
        tiles[c * TILES + 120:(c + 1) * TILES, :] = jnp.zeros((TILES - 120, LANES), F32)


def load_part(part, tiles, groups):
    for m in range(GRP * groups[1]):
        at = (GRP * groups[0] + m) * TILES
        tiles[at:at + LANES, :] = part[m].astype(F32)


def store_part(tiles, part, groups):
    for m in range(GRP * groups[1]):
        at = (GRP * groups[0] + m) * TILES
        part[m] = tiles[at:at + LANES, :].astype(BF16)


def update_kernel(steps, source, result, groups, count, noted, *refs):
    env, sites, operator = refs[0], refs[1:1 + len(steps)], refs[1 + len(steps)]
    note = refs[2 + len(steps)] if noted else None
    refs = refs[count:]
    out, tiles, rows, rows_a, spread_a, middle = refs[:6]
    blocks = refs[6:6 + len(sites)]
    if steps[0] == "L":
        widen(operator, *refs[7 + len(sites):])
        operator = refs[7 + len(sites)]
    if source != "rows":
        clear_tails(tiles)
        (load_raw if source == "raw" else load_wire)(env, tiles, *([ENV // LANES] if source == "raw" else []))
    else:
        rows[WD * BLK:, :] = jnp.zeros(((WPAD - WD) * BLK, LANES), F32)
    for site, block in zip(sites, blocks):
        load_sites(site, block)

    def one(local, carry):
        group = local + groups[0]
        if source == "rows":
            rows[:WD * BLK, :] = env[local].astype(F32)
        else:
            flat_to_rows(tiles, group, 48, rows)
        for step, block in zip(steps, blocks):
            site_rows(block, group, rows_a, spread_a)
            (left_step if step == "L" else right_step)(rows, rows_a, spread_a, operator, middle, refs[6 + len(sites)])
        if result == "rows":
            out[local] = rows[:WD * BLK, :].astype(BF16)
        else:
            rows_to_flat(rows, group, 48, tiles)
        return carry

    lax.fori_loop(0, groups[1], one, 0)
    if result == "part":
        store_part(tiles, out, groups)
    elif result == "raw":
        store_raw(tiles, out, ENV // LANES)
    elif result == "wire":
        if noted:
            tiles[pl.ds(126, SEC, stride=TILES), :] = note[...].astype(F32)
        store_wire(tiles, out)


def update(steps, source, result, groups, env, sites, operator, note=None, *tickets):
    shape = {"rows": (groups[1], WD * BLK, LANES), "part": (GRP * groups[1], LANES, LANES), "wire": (16, 160, LANES), "raw": (SEC, ENV)}[result]
    middle = (WD, 96, LANES) if steps[0] == "L" else (12, 224, LANES)
    inputs = [env, *sites, operator] + ([] if note is None else [note]) + list(tickets)
    return pl.pallas_call(
        functools.partial(update_kernel, steps, source, result, groups, len(inputs), note is not None),
        out_shape=jax.ShapeDtypeStruct(shape, BF16),
        in_specs=[pl.BlockSpec(memory_space=pltpu.VMEM)] * (len(inputs) - len(tickets)) + [pl.BlockSpec(memory_space=pl.ANY)] * len(tickets),
        out_specs=pl.BlockSpec(memory_space=pltpu.VMEM),
        scratch_shapes=[
            pltpu.VMEM((SEC * TILES, LANES), F32),
            pltpu.VMEM((WPAD * BLK, LANES), F32),
            pltpu.VMEM((LANES, LANES), F32),
            pltpu.VMEM((PHYS * BLK, LANES), F32),
            pltpu.VMEM(middle, BF16),
        ] + [pltpu.VMEM((SEC * 24, LANES), F32)] * len(sites)
        + ([pltpu.VMEM((6, 256, 256), BF16), pltpu.VMEM((WD * 8, 2 * LANES), BF16), pltpu.VMEM((2 * WD * 8, LANES), F32)]
           if steps[0] == "L" else [pltpu.VMEM((WPAD * BLK, 4 * LANES), BF16)]),
        compiler_params=pltpu.CompilerParams(vmem_limit_bytes=16 * 1024 * 1024),
        cost_estimate=pl.CostEstimate(flops=(2000000000 if steps[0] == "L" else 50000000) * groups[1] * len(sites), bytes_accessed=100000, transcendentals=0),
        name="update_" + "".join(steps).lower() + str(groups[0]),
    )(*inputs)


def left_operator(op):
    return jnp.pad(op.transpose(1, 2, 3, 0), ((0, 0), (0, 0), (0, 0), (0, WPAD - WD))).reshape(WD * PHYS, LANES).astype(F32)


def right_operator(op):
    same = jnp.eye(2, dtype=BF16)
    wide = jnp.pad(op, ((0, WPAD - WD), (0, 0), (0, 0), (0, 0)))
    return jnp.einsum("wvts,ab->tawvbs", wide, same).reshape(8 * WPAD, WD * 8)


def call(kernel, name, shapes, inputs, scratch, in_smem=0):
    spaces = [pltpu.SMEM] * in_smem + [pltpu.VMEM] * (len(inputs) - in_smem)
    return pl.pallas_call(
        kernel,
        out_shape=[jax.ShapeDtypeStruct(shape, BF16) for shape in shapes],
        in_specs=[pl.BlockSpec(memory_space=space) for space in spaces],
        out_specs=[pl.BlockSpec(memory_space=pltpu.VMEM)] * len(shapes),
        scratch_shapes=scratch,
        compiler_params=pltpu.CompilerParams(vmem_limit_bytes=16 * 1024 * 1024),
        cost_estimate=pl.CostEstimate(flops=2000000000, bytes_accessed=100000, transcendentals=0),
        name=name,
    )(*inputs)


def wire_kernel(raw, out, tiles):
    clear_tails(tiles)
    load_raw(raw, tiles, ENV // LANES)
    store_wire(tiles, out)


def to_wire(raw):
    return call(wire_kernel, "to_wire", [(16, 160, LANES)], [raw], [pltpu.VMEM((SEC * TILES, LANES), F32)])[0]


def permute_wire(order, wire, out, held):
    for q in range(16):
        for m in range(SEC // 2):
            at = (q * SEC + 2 * m) * 8
            held[at:at + 16, :] = wire[q, 16 * m:16 * m + 16, :].astype(F32)
    for q in range(16):
        for m in range(SEC // 2):
            pair = [held[pl.ds(pl.multiple_of(order[q * SEC + 2 * m + h] * 8, 8), 8), :] for h in range(2)]
            out[q, 16 * m:16 * m + 16, :] = jnp.concatenate(pair, 0).astype(BF16)


def permute_pack_kernel(order, chosen, wire, sites, sites1, out, held, block, block1):
    permute_wire(order, wire, out, held)
    load_sites(sites, block)
    load_sites(sites1, block1)
    for q in range(16):
        for n, source in enumerate((block, block1)):
            pair = [source[pl.ds(pl.multiple_of(chosen[32 * n + 2 * q + h] * 24, 8), 24), :] for h in range(2)]
            out[q, 160 + 48 * n:208 + 48 * n, :] = jnp.concatenate(pair, 0).astype(BF16)


def permute_pack(order, chosen, wire, sites, sites1):
    scratch = [pltpu.VMEM((16 * 160, LANES), F32)] + [pltpu.VMEM((SEC * 24, LANES), F32)] * 2
    return call(permute_pack_kernel, "permute_pack", [(16, 256, LANES)], [order, chosen, wire, sites, sites1], scratch, 2)[0]


def fetch_kernel(places, wire, fetched, pushed, extra):
    for q in range(16):
        extra[q * 96:q * 96 + 96, :] = wire[q, 160:256, :].astype(F32)
    for n, out in enumerate((fetched, pushed)):
        for m in range(SEC // 2):
            pair = [extra[pl.ds(pl.multiple_of(places[SEC * n + 2 * m + h] * 24, 8), 24), :] for h in range(2)]
            out[48 * m:48 * m + 48, :] = jnp.concatenate(pair, 0).astype(BF16)


def fetch(places, wire):
    return call(fetch_kernel, "fetch", [(SEC * 24, LANES)] * 2, [places, wire], [pltpu.VMEM((16 * 96, LANES), F32)], 1)


def touch_kernel(value, out):
    out[...] = jnp.zeros((16, LANES), BF16)


def touch(value):
    return pl.pallas_call(
        touch_kernel,
        out_shape=jax.ShapeDtypeStruct((16, LANES), BF16),
        in_specs=[pl.BlockSpec(memory_space=pl.ANY)],
        out_specs=pl.BlockSpec(memory_space=pltpu.VMEM),
        cost_estimate=pl.CostEstimate(flops=20000000000, bytes_accessed=1000, transcendentals=0),
        name="touch",
    )(value)


def permute(order, wire):
    return call(permute_wire, "permute", [(16, 160, LANES)], [order, wire], [pltpu.VMEM((16 * 160, LANES), F32)], 1)[0]


def join_kernel(first, second, out, tiles):
    load_part(first, tiles, FIRST)
    load_part(second, tiles, SECOND)
    store_raw(tiles, out, ENV // LANES)


def join(first, second):
    return call(join_kernel, "join", [(SEC, ENV)], [first, second], [pltpu.VMEM((SEC * TILES, LANES), F32)])[0]


def shifted(x, by):
    length = lax.axis_size("blk")
    return lax.ppermute(x, "blk", [(i, (i + by) % length) for i in range(length)])


def exchanged(x):
    return lax.all_to_all(x, "panel", split_axis=0, concat_axis=0, tiled=True)


def after(x, *others):
    return lax.optimization_barrier((x, *others))[0]


def pick(values, index):
    hits = index[:, None] == jnp.arange(values.shape[0])[None, :]
    return jnp.sum(jnp.where(hits, values[None, :], 0), axis=1)


def right_order(c0, s0, c1, s1):
    panels = jnp.arange(16)[:, None]
    offset, slot = c1 + pick(c0, s1), pick(s0, s1)
    return ((panels + offset[None, :]) % 16 * SEC + slot[None, :]).reshape(-1)


def left_order(c1, s1, c2, s2):
    panels = jnp.arange(16)[:, None]
    offset, slot = c2 + pick(c1, s2), pick(s1, s2)
    hits = jnp.arange(SEC)[:, None] == slot[None, :]
    source = jnp.sum(jnp.where(hits, jnp.arange(SEC)[None, :], 0), axis=1)
    back = jnp.sum(jnp.where(hits, offset[None, :], 0), axis=1)
    return ((panels - back[None, :]) % 16 * SEC + source[None, :]).reshape(-1)


def move_plan(me, c1, s1):
    slots = jnp.arange(SEC)
    rank = jnp.sum((c1[None, :] == c1[:, None]) & (slots[None, :] < slots[:, None]), axis=1)
    place = jnp.arange(32)
    same = (place % 2)[:, None] == rank[None, :]
    asked = same & (((me - place // 2) % 16)[:, None] == c1[None, :])
    pushed = same & (((place // 2 - me) % 16)[:, None] == c1[None, :])
    chosen = [jnp.sum(jnp.where(asked, s1[None, :], 0), axis=1), jnp.sum(jnp.where(pushed, slots[None, :], 0), axis=1)]
    landing = slots[:, None] == s1[None, :]
    back = jnp.sum(jnp.where(landing, ((me - c1) % 16 * 4 + 2 + rank)[None, :], 0), axis=1)
    return jnp.concatenate(chosen), jnp.concatenate([(me + c1) % 16 * 4 + rank, back])


def masked(tensor, rows, cols, noted):
    place = jnp.arange(tensor.shape[1] + LANES)
    live = place < tensor.shape[1]
    keep = live & ((place // BLK % BLK)[None, :] < rows[:, None]) & ((place % BLK)[None, :] < cols[:, None])
    tensor = jnp.pad(tensor, ((0, 0), (0, LANES)))
    extra = jnp.where(place == SITE, (noted // SEC)[:, None], jnp.where(place == SITE + 1, (noted % SEC)[:, None], 0))
    return jnp.where(keep, tensor, extra.astype(BF16))


def body(left_env, right_env, site_tensors, chain_operator, targets, sector_dims):
    me = lax.axis_index("panel")
    wire = to_wire(right_env[0])
    arrived = exchanged(wire)

    target = targets[0]
    code = (target // SEC - me) % 16 * SEC + target % SEC
    rows = lax.dynamic_slice_in_dim(sector_dims, me * SEC, SEC)
    blocks = after(masked(site_tensors[0], rows, pick(sector_dims, target), code), wire)
    blocks1 = shifted(blocks, 1)
    operator = left_operator(after(chain_operator, wire))
    left = update(("L",), "raw", "wire", WHOLE, left_env[0], [blocks], operator, blocks[:, SITE:])
    left_moved = shifted(left, 2)

    noted = blocks1[:, SITE:SITE + 2].astype(jnp.int32)
    c0, s0, c1, s1 = code // SEC, code % SEC, noted[:, 0], noted[:, 1]
    chosen, places = move_plan(me, c1, s1)
    wire = permute_pack(right_order(c0, s0, c1, s1), chosen, after(arrived, left), blocks, blocks1)
    right = exchanged(wire)
    fetched, pushed = fetch(places, right)

    operator_r = right_operator(after(chain_operator, wire))
    left = exchanged(after(left_moved, fetched))
    right0 = update(("R", "R"), "wire", "part", FIRST, right, [fetched, blocks1], operator_r, None, touch(left_moved))
    right0_moved = shifted(right0, -2)
    noted = after(left_moved, fetched)[15].reshape(SEC, 8, LANES)[:, 6, :2].astype(jnp.int32)
    ordered = permute(left_order(c1, s1, noted[:, 0], noted[:, 1]), left)
    left = exchanged(ordered)
    right1 = update(("R", "R"), "wire", "part", SECOND, after(right, right0, ordered), [fetched, blocks1], operator_r)
    right1_moved = shifted(right1, -2)
    left_out = update(("L",), "wire", "raw", WHOLE, left, [pushed], operator, None, touch(after(right0_moved, right1)))
    right_out = join(after(right0_moved, left_out), right1_moved)
    return left_out[None], right_out[None]


def solution(mesh):
    whole = P("blk", "panel", None)
    return jax.shard_map(
        body,
        mesh=mesh,
        in_specs=(whole, whole, whole, P(), P("blk", "panel"), P()),
        out_specs=(whole, whole),
        check_vma=False,
    )
```

```python
import functools
import jax
import jax.numpy as jnp
from jax import lax
from jax.experimental import pallas as pl
from jax.experimental.pallas import tpu as pltpu
from jax.sharding import PartitionSpec as P

WD, PHYS, BLK = 28, 4, 24
WPAD = 32
SEC = 20
PIECES, WHOLE = ((0, 2), (2, 2)), (0, 4)
GRP = 5
LANES = 128
TILES = 144
ENV = WD * BLK * BLK
SITE = PHYS * BLK * BLK
F32, BF16 = jnp.float32, jnp.bfloat16


def lane_ids(rows):
    return lax.broadcasted_iota(jnp.int32, (rows, LANES), 1)


def between(lane, low, high):
    return (lane >= low) & (lane < high)


def spans(b):
    out = []
    for r in range(3):
        low, high = max(24 * b - LANES * r, 0), min(24 * b + 24 - LANES * r, LANES)
        if low < high:
            out.append((r, low, high))
    return out


def merge(lane, pieces):
    acc = None
    for value, low, high in pieces:
        acc = value if acc is None else jnp.where(between(lane, low, high), value, acc)
    return acc


def turned(value, shift):
    return pltpu.roll(value, shift % LANES, 1) if shift % LANES else value


def flat_to_rows(tiles, group, steps, rows):
    lane = lane_ids(steps)
    live = lane < GRP * BLK
    shifted_by = {}

    def source(c, r):
        return tiles[pl.ds((group * GRP + c) * 3 * steps + r, steps, stride=3), :]

    for b in range(16):
        for d in range(-b, GRP - b):
            if d not in shifted_by:
                pieces = [(source(c, r), low, high) for c in range(GRP) if 0 <= c - d < 16 for r, low, high in spans(c - d)]
                shifted_by[d] = turned(merge(lane, pieces), 24 * d)
        acc = merge(lane, [(shifted_by[c - b], 24 * c, 24 * c + 24) for c in range(GRP)])
        rows[pl.ds(b, steps, stride=16), :] = jnp.where(live, acc, 0.0)
        del shifted_by[GRP - 1 - b]


def rows_to_flat(rows, group, steps, tiles):
    lane = lane_ids(steps)
    for r in range(3):
        shifted_by = {}
        inside = [(b, low, high) for b in range(16) for tile, low, high in spans(b) if tile == r]
        for c in range(GRP):
            pieces = []
            for b, low, high in inside:
                d = c - b
                if d not in shifted_by:
                    parts = [(rows[pl.ds(e - d, steps, stride=16), :], 24 * e, 24 * e + 24) for e in range(GRP) if 0 <= e - d < 16]
                    shifted_by[d] = turned(merge(lane, parts), -24 * d)
                pieces.append((shifted_by[d], low, high))
            tiles[pl.ds((group * GRP + c) * 3 * steps + r, steps, stride=3), :] = merge(lane, pieces)


def load_raw(raw, tiles, count):
    pad = tiles.shape[0] // SEC
    for n in range(count):
        tiles[pl.ds(n, SEC, stride=pad), :] = raw[:, n * LANES:(n + 1) * LANES].astype(F32)


def store_raw(tiles, raw, count):
    pad = tiles.shape[0] // SEC
    for n in range(count):
        raw[:, n * LANES:(n + 1) * LANES] = tiles[pl.ds(n, SEC, stride=pad), :].astype(BF16)


def load_wire(wire, tiles):
    for q in range(16):
        for m in range(SEC // 2):
            pair = wire[q, 16 * m:16 * m + 16, :].astype(F32)
            at = 2 * m * TILES + 8 * q
            tiles[at:at + 8, :] = pair[:8]
            tiles[at + TILES:at + TILES + 8, :] = pair[8:]


def store_wire(tiles, wire):
    for q in range(16):
        for m in range(SEC // 2):
            at = 2 * m * TILES + 8 * q
            pair = jnp.concatenate([tiles[at:at + 8, :], tiles[at + TILES:at + TILES + 8, :]], 0)
            wire[q, 16 * m:16 * m + 16, :] = pair.astype(BF16)


def site_rows(blocks, group, rows, spread):
    flat_to_rows(blocks, group, 8, rows)
    for s in range(PHYS):
        spread[pl.ds(s, BLK, stride=PHYS), :] = rows[s * BLK:(s + 1) * BLK, :]


def diagonal(rows, s):
    lane = lane_ids(BLK)
    block = rows[s * BLK:(s + 1) * BLK, :]
    parts = [jnp.where(between(lane, 24 * c, 24 * c + 24), block, 0.0) for c in range(GRP)]
    parts.append(jnp.zeros((8, LANES), F32))
    return jnp.concatenate(parts, 0)


def widen(operator, wide, held):
    held[...] = jnp.zeros((2 * WD * 8, LANES), F32)
    for t in range(PHYS):
        value = operator[pl.ds(t, WD, stride=PHYS), :]
        for i in range(2):
            held[pl.ds(WD * 8 * i + PHYS * i + t, WD, stride=8), :] = value
    wide[...] = jnp.concatenate([held[:WD * 8, :], held[WD * 8:, :]], 1).astype(BF16)


def left_step(rows, rows_a, spread_a, operator, middle, spread):
    diag = jnp.concatenate([diagonal(rows_a, s) for s in range(PHYS)], 1).astype(BF16)
    last = spread_a[...].T.astype(BF16)
    env = jnp.concatenate([rows[pl.ds(d, WPAD, stride=BLK), :] for d in range(BLK)], 0).astype(BF16)
    xs = jnp.dot(env, diag, preferred_element_type=F32).astype(BF16)
    for p in range(6):
        x = xs[128 * p:128 * p + 128]
        for n in range(2):
            for s in range(PHYS):
                at = (4 * n + s) * WPAD
                spread[p, at:at + WPAD, :LANES] = x[n * WPAD:(n + 1) * WPAD, s * LANES:(s + 1) * LANES]
                spread[p, at:at + WPAD, LANES:] = x[64 + n * WPAD:64 + (n + 1) * WPAD, s * LANES:(s + 1) * LANES]
    for p in range(6):
        y = jnp.dot(operator[...], spread[p], preferred_element_type=F32)
        even = y[:, :LANES].reshape(WD, 8, LANES)
        odd = y[:, LANES:].reshape(WD, 8, LANES)
        middle[:, 16 * p:16 * p + 16, :] = jnp.concatenate([even, odd], 1).astype(BF16)
    lane = lane_ids(BLK)
    for u in range(WD // 2):
        y = jnp.concatenate([middle[2 * u], middle[2 * u + 1]], 1)
        out = jnp.dot(last, y, preferred_element_type=F32)
        for h in range(2):
            half = out[:, h * LANES:(h + 1) * LANES]
            acc = jnp.zeros((BLK, LANES), F32)
            for c in range(GRP):
                acc = jnp.where(between(lane, 24 * c, 24 * c + 24), half[24 * c:24 * c + 24], acc)
            rows[(2 * u + h) * BLK:(2 * u + h + 1) * BLK, :] = acc


def right_step(rows, rows_a, spread_a, operator, middle, spread):
    first = spread_a[...].astype(BF16)
    diag = jnp.concatenate([diagonal(rows_a, s).T for s in range(PHYS)], 0).astype(BF16)
    lane = lane_ids(BLK)
    zeros = jnp.zeros((8, LANES), F32)
    for u in range(WD // 2):
        halves = []
        for h in range(2):
            block = rows[(2 * u + h) * BLK:(2 * u + h + 1) * BLK, :]
            parts = [jnp.where(between(lane, 24 * c, 24 * c + 24), block, 0.0) for c in range(GRP)]
            halves.append(jnp.concatenate(parts + [zeros], 0))
        z = jnp.dot(first, jnp.concatenate(halves, 1).astype(BF16), preferred_element_type=F32)
        even = z[:, :LANES].reshape(12, 8, LANES)
        odd = z[:, LANES:].reshape(12, 8, LANES)
        middle[:, 16 * u:16 * u + 16, :] = jnp.concatenate([even, odd], 1).astype(BF16)
    for p in range(6):
        z = jnp.concatenate([middle[2 * p], middle[2 * p + 1]], 1)
        v = jnp.dot(operator[...], z, preferred_element_type=F32).astype(BF16)
        for h in range(2):
            for t in range(PHYS):
                spread[LANES * p + 64 * h:LANES * p + 64 * h + 64, t * LANES:(t + 1) * LANES] = v[64 * t:64 * t + 64, h * LANES:(h + 1) * LANES]
    out = jnp.dot(spread[...], diag, preferred_element_type=F32)
    for d in range(BLK):
        rows[pl.ds(d, WPAD, stride=BLK), :] = out[d * WPAD:(d + 1) * WPAD, :]


def load_sites(site, block):
    if site.shape[0] == SEC:
        for c in range(SEC):
            block[c * 24 + 16:c * 24 + 24, :] = jnp.zeros((8, LANES), F32)
        load_raw(site, block, 18)
    else:
        block[...] = site[...].astype(F32)


def clear_tails(tiles):
    for c in range(SEC):
        tiles[c * TILES + 120:(c + 1) * TILES, :] = jnp.zeros((TILES - 120, LANES), F32)


def load_part(part, tiles, groups):
    for m in range(GRP * groups[1]):
        at = (GRP * groups[0] + m) * TILES
        tiles[at:at + LANES, :] = part[m].astype(F32)


def store_part(tiles, part, groups):
    for m in range(GRP * groups[1]):
        at = (GRP * groups[0] + m) * TILES
        part[m] = tiles[at:at + LANES, :].astype(BF16)


def update_kernel(steps, source, result, groups, count, noted, *refs):
    env, sites, operator = refs[0], refs[1:1 + len(steps)], refs[1 + len(steps)]
    note = refs[2 + len(steps)] if noted else None
    refs = refs[count:]
    out, tiles, rows, rows_a, spread_a, middle = refs[:6]
    blocks = refs[6:6 + len(sites)]
    if steps[0] == "L":
        widen(operator, *refs[7 + len(sites):])
        operator = refs[7 + len(sites)]
    if source != "rows":
        clear_tails(tiles)
        (load_raw if source == "raw" else load_wire)(env, tiles, *([ENV // LANES] if source == "raw" else []))
    else:
        for local in range(groups[1]):
            rows[local, WD * BLK:, :] = jnp.zeros(((WPAD - WD) * BLK, LANES), F32)
    for site, block in zip(sites, blocks):
        load_sites(site, block)

    def enter(local):
        if source == "rows":
            rows.at[local][:WD * BLK, :] = env[local].astype(F32)
        else:
            flat_to_rows(tiles, local + groups[0], 48, rows.at[local])
        for n, block in enumerate(blocks):
            site_rows(block, local + groups[0], rows_a.at[local, n], spread_a.at[local, n])

    def leave(local):
        if result == "rows":
            out[local] = rows.at[local][:WD * BLK, :].astype(BF16)
        else:
            rows_to_flat(rows.at[local], local + groups[0], 48, tiles)

    enter(0)
    for local in range(groups[1]):
        if local + 1 < groups[1]:
            enter(local + 1)
        for n, step in enumerate(steps):
            (left_step if step == "L" else right_step)(
                rows.at[local], rows_a.at[local, n], spread_a.at[local, n], operator, middle.at[local % 2], refs[6 + len(sites)])
        if local > 0:
            leave(local - 1)
    leave(groups[1] - 1)
    if result == "part":
        store_part(tiles, out, groups)
    elif result == "raw":
        store_raw(tiles, out, ENV // LANES)
    elif result == "wire":
        if noted:
            tiles[pl.ds(126, SEC, stride=TILES), :] = note[...].astype(F32)
        store_wire(tiles, out)


def update(steps, source, result, groups, env, sites, operator, note=None, *tickets):
    shape = {"rows": (groups[1], WD * BLK, LANES), "part": (GRP * groups[1], LANES, LANES), "wire": (16, 160, LANES), "raw": (SEC, ENV)}[result]
    middle = (WD, 96, LANES) if steps[0] == "L" else (12, 224, LANES)
    inputs = [env, *sites, operator] + ([] if note is None else [note]) + list(tickets)
    return pl.pallas_call(
        functools.partial(update_kernel, steps, source, result, groups, len(inputs), note is not None),
        out_shape=jax.ShapeDtypeStruct(shape, BF16),
        in_specs=[pl.BlockSpec(memory_space=pltpu.VMEM)] * (len(inputs) - len(tickets)) + [pl.BlockSpec(memory_space=pl.ANY)] * len(tickets),
        out_specs=pl.BlockSpec(memory_space=pltpu.VMEM),
        scratch_shapes=[
            pltpu.VMEM((SEC * TILES, LANES), F32),
            pltpu.VMEM((groups[1], WPAD * BLK, LANES), F32),
            pltpu.VMEM((groups[1], len(sites), LANES, LANES), F32),
            pltpu.VMEM((groups[1], len(sites), PHYS * BLK, LANES), F32),
            pltpu.VMEM((2,) + middle, BF16),
        ] + [pltpu.VMEM((SEC * 24, LANES), F32)] * len(sites)
        + ([pltpu.VMEM((6, 256, 256), BF16), pltpu.VMEM((WD * 8, 2 * LANES), BF16), pltpu.VMEM((2 * WD * 8, LANES), F32)]
           if steps[0] == "L" else [pltpu.VMEM((WPAD * BLK, 4 * LANES), BF16)]),
        compiler_params=pltpu.CompilerParams(vmem_limit_bytes=16 * 1024 * 1024),
        cost_estimate=pl.CostEstimate(flops=(2000000000 if steps[0] == "L" else 50000000) * groups[1] * len(sites), bytes_accessed=100000, transcendentals=0),
        name="update_" + "".join(steps).lower() + str(groups[0]),
    )(*inputs)


def left_operator(op):
    return jnp.pad(op.transpose(1, 2, 3, 0), ((0, 0), (0, 0), (0, 0), (0, WPAD - WD))).reshape(WD * PHYS, LANES).astype(F32)


def right_operator(op):
    same = jnp.eye(2, dtype=BF16)
    wide = jnp.pad(op, ((0, WPAD - WD), (0, 0), (0, 0), (0, 0)))
    return jnp.einsum("wvts,ab->tawvbs", wide, same).reshape(8 * WPAD, WD * 8)


def call(kernel, name, shapes, inputs, scratch, in_smem=0):
    spaces = [pltpu.SMEM] * in_smem + [pltpu.VMEM] * (len(inputs) - in_smem)
    return pl.pallas_call(
        kernel,
        out_shape=[jax.ShapeDtypeStruct(shape, BF16) for shape in shapes],
        in_specs=[pl.BlockSpec(memory_space=space) for space in spaces],
        out_specs=[pl.BlockSpec(memory_space=pltpu.VMEM)] * len(shapes),
        scratch_shapes=scratch,
        compiler_params=pltpu.CompilerParams(vmem_limit_bytes=16 * 1024 * 1024),
        cost_estimate=pl.CostEstimate(flops=2000000000, bytes_accessed=100000, transcendentals=0),
        name=name,
    )(*inputs)


def wire_kernel(raw, out, tiles):
    clear_tails(tiles)
    load_raw(raw, tiles, ENV // LANES)
    store_wire(tiles, out)


def to_wire(raw):
    return call(wire_kernel, "to_wire", [(16, 160, LANES)], [raw], [pltpu.VMEM((SEC * TILES, LANES), F32)])[0]


def permute_wire(order, wire, out, held):
    for q in range(16):
        for m in range(SEC // 2):
            at = (q * SEC + 2 * m) * 8
            held[at:at + 16, :] = wire[q, 16 * m:16 * m + 16, :].astype(F32)
    for q in range(16):
        for m in range(SEC // 2):
            pair = [held[pl.ds(pl.multiple_of(order[q * SEC + 2 * m + h] * 8, 8), 8), :] for h in range(2)]
            out[q, 16 * m:16 * m + 16, :] = jnp.concatenate(pair, 0).astype(BF16)


def permute_pack_kernel(order, chosen, wire, sites, out, held, block):
    permute_wire(order, wire, out, held)
    load_sites(sites, block)
    for q in range(16):
        pair = [block[pl.ds(pl.multiple_of(chosen[2 * q + h] * 24, 8), 24), :] for h in range(2)]
        out[q, 160:208, :] = jnp.concatenate(pair, 0).astype(BF16)


def permute_pack(order, chosen, wire, sites):
    scratch = [pltpu.VMEM((16 * 160, LANES), F32), pltpu.VMEM((SEC * 24, LANES), F32)]
    return call(permute_pack_kernel, "permute_pack", [(16, 208, LANES)], [order, chosen, wire, sites], scratch, 2)[0]


def fetch_kernel(places, wire, fetched, extra):
    for q in range(16):
        extra[q * 48:q * 48 + 48, :] = wire[q, 160:208, :].astype(F32)
    for m in range(SEC // 2):
        pair = [extra[pl.ds(pl.multiple_of(places[2 * m + h] * 24, 8), 24), :] for h in range(2)]
        fetched[48 * m:48 * m + 48, :] = jnp.concatenate(pair, 0).astype(BF16)


def fetch(places, wire):
    return call(fetch_kernel, "fetch", [(SEC * 24, LANES)], [places, wire], [pltpu.VMEM((16 * 48, LANES), F32)], 1)[0]


def touch_kernel(*refs):
    refs[-1][...] = jnp.zeros((16, LANES), BF16)


def touch(*values):
    return pl.pallas_call(
        touch_kernel,
        out_shape=jax.ShapeDtypeStruct((16, LANES), BF16),
        in_specs=[pl.BlockSpec(memory_space=pl.ANY)] * len(values),
        out_specs=pl.BlockSpec(memory_space=pltpu.VMEM),
        cost_estimate=pl.CostEstimate(flops=20000000000, bytes_accessed=1000, transcendentals=0),
        name="touch",
    )(*values)


def join_kernel(*refs):
    parts, out, tiles = refs[:-2], refs[-2], refs[-1]
    for part, groups in zip(parts, PIECES):
        load_part(part, tiles, groups)
    store_raw(tiles, out, ENV // LANES)


def join(*parts):
    return call(join_kernel, "join", [(SEC, ENV)], parts, [pltpu.VMEM((SEC * TILES, LANES), F32)])[0]


def shifted(x, by):
    length = lax.axis_size("blk")
    return lax.ppermute(x, "blk", [(i, (i + by) % length) for i in range(length)])


def exchanged(x):
    return lax.all_to_all(x, "panel", split_axis=0, concat_axis=0, tiled=True)


def after(x, *others):
    return lax.optimization_barrier((x, *others))[0]


def pick(values, index):
    hits = index[:, None] == jnp.arange(values.shape[0])[None, :]
    return jnp.sum(jnp.where(hits, values[None, :], 0), axis=1)


def right_order(c0, s0, c1, s1):
    panels = jnp.arange(16)[:, None]
    offset, slot = c1 + pick(c0, s1), pick(s0, s1)
    return ((panels + offset[None, :]) % 16 * SEC + slot[None, :]).reshape(-1)


def left_order(c1, s1, c2, s2):
    panels = jnp.arange(16)[:, None]
    offset, slot = c2 + pick(c1, s2), pick(s1, s2)
    hits = jnp.arange(SEC)[:, None] == slot[None, :]
    source = jnp.sum(jnp.where(hits, jnp.arange(SEC)[None, :], 0), axis=1)
    back = jnp.sum(jnp.where(hits, offset[None, :], 0), axis=1)
    return ((panels - back[None, :]) % 16 * SEC + source[None, :]).reshape(-1)


def move_plan(me, c1, s1):
    slots = jnp.arange(SEC)
    rank = jnp.sum((c1[None, :] == c1[:, None]) & (slots[None, :] < slots[:, None]), axis=1)
    place = jnp.arange(32)
    same = (place % 2)[:, None] == rank[None, :]
    asked = same & (((me - place // 2) % 16)[:, None] == c1[None, :])
    pushed = same & (((place // 2 - me) % 16)[:, None] == c1[None, :])
    chosen = [jnp.sum(jnp.where(asked, s1[None, :], 0), axis=1), jnp.sum(jnp.where(pushed, slots[None, :], 0), axis=1)]
    landing = slots[:, None] == s1[None, :]
    back = jnp.sum(jnp.where(landing, ((me - c1) % 16 * 2 + rank)[None, :], 0), axis=1)
    return chosen, [(me + c1) % 16 * 2 + rank, back]


def masked(tensor, rows, cols, noted):
    place = jnp.arange(tensor.shape[1] + LANES)
    live = place < tensor.shape[1]
    keep = live & ((place // BLK % BLK)[None, :] < rows[:, None]) & ((place % BLK)[None, :] < cols[:, None])
    tensor = jnp.pad(tensor, ((0, 0), (0, LANES)))
    extra = jnp.where(place == SITE, (noted // SEC)[:, None], jnp.where(place == SITE + 1, (noted % SEC)[:, None], 0))
    return jnp.where(keep, tensor, extra.astype(BF16))


def body(left_env, right_env, site_tensors, chain_operator, targets, sector_dims):
    me = lax.axis_index("panel")
    wire = to_wire(right_env[0])
    arrived = exchanged(wire)

    target = targets[0]
    code = (target // SEC - me) % 16 * SEC + target % SEC
    rows = lax.dynamic_slice_in_dim(sector_dims, me * SEC, SEC)
    blocks = after(masked(site_tensors[0], rows, pick(sector_dims, target), code), wire)
    blocks1 = shifted(blocks, 1)
    operator = left_operator(after(chain_operator, wire))
    left = update(("L",), "raw", "wire", WHOLE, left_env[0], [blocks], operator, blocks[:, SITE:])
    left_moved = shifted(left, 2)

    noted = blocks1[:, SITE:SITE + 2].astype(jnp.int32)
    c0, s0, c1, s1 = code // SEC, code % SEC, noted[:, 0], noted[:, 1]
    chosen, places = move_plan(me, c1, s1)
    wire = permute_pack(right_order(c0, s0, c1, s1), chosen[0], after(arrived, left), blocks)
    right = exchanged(wire)
    fetched = fetch(places[0], right)

    operator_r = right_operator(after(chain_operator, wire))
    left = exchanged(after(left_moved, fetched))
    def right_piece(number, *order):
        tickets = [touch(left_moved)] if number == 0 else []
        piece = update(("R", "R"), "wire", "part", PIECES[number], after(right, *order), [fetched, blocks1], operator_r, None, *tickets)
        return piece, shifted(piece, -2)

    right0, moved0 = right_piece(0)
    noted = after(left_moved, right0)[15].reshape(SEC, 8, LANES)[:, 6, :2].astype(jnp.int32)
    ordered = permute_pack(left_order(c1, s1, noted[:, 0], noted[:, 1]), chosen[1], left, blocks1)
    left = exchanged(ordered)
    right1, moved1 = right_piece(1, right0, ordered)
    left_out = update(("L",), "wire", "raw", WHOLE, left, [fetch(places[1], left)], operator, None, touch(after(moved0, right1)))
    right_out = join(after(moved0, left_out), moved1)
    return left_out[None], right_out[None]


def solution(mesh):
    whole = P("blk", "panel", None)
    return jax.shard_map(
        body,
        mesh=mesh,
        in_specs=(whole, whole, whole, P(), P("blk", "panel"), P()),
        out_specs=(whole, whole),
        check_vma=False,
    )
```

```python
import functools
import jax
import jax.numpy as jnp
from jax import lax
from jax.experimental import pallas as pl
from jax.experimental.pallas import tpu as pltpu
from jax.sharding import PartitionSpec as P

WD, PHYS, BLK = 28, 4, 24
WPAD = 32
SEC = 20
ROOM = 24
PIECES, WHOLE = ((0, 2), (2, 2)), (0, 4)
GRP = 5
LANES = 128
TILES = 144
ENV = WD * BLK * BLK
SITE = PHYS * BLK * BLK
F32, BF16 = jnp.float32, jnp.bfloat16


def lane_ids(rows):
    return lax.broadcasted_iota(jnp.int32, (rows, LANES), 1)


def between(lane, low, high):
    return (lane >= low) & (lane < high)


def spans(b):
    out = []
    for r in range(3):
        low, high = max(24 * b - LANES * r, 0), min(24 * b + 24 - LANES * r, LANES)
        if low < high:
            out.append((r, low, high))
    return out


def merge(lane, pieces):
    acc = None
    for value, low, high in pieces:
        acc = value if acc is None else jnp.where(between(lane, low, high), value, acc)
    return acc


def turned(value, shift):
    return pltpu.roll(value, shift % LANES, 1) if shift % LANES else value


def flat_to_rows(tiles, group, steps, rows):
    lane = lane_ids(steps)
    live = lane < GRP * BLK
    shifted_by = {}

    def source(c, r):
        return tiles[pl.ds((group * GRP + c) * 3 * steps + r, steps, stride=3), :]

    for b in range(16):
        for d in range(-b, GRP - b):
            if d not in shifted_by:
                pieces = [(source(c, r), low, high) for c in range(GRP) if 0 <= c - d < 16 for r, low, high in spans(c - d)]
                shifted_by[d] = turned(merge(lane, pieces), 24 * d)
        acc = merge(lane, [(shifted_by[c - b], 24 * c, 24 * c + 24) for c in range(GRP)])
        rows[pl.ds(b, steps, stride=16), :] = jnp.where(live, acc, 0.0)
        del shifted_by[GRP - 1 - b]


def rows_to_flat(rows, group, steps, tiles):
    lane = lane_ids(steps)
    for r in range(3):
        shifted_by = {}
        inside = [(b, low, high) for b in range(16) for tile, low, high in spans(b) if tile == r]
        for c in range(GRP):
            pieces = []
            for b, low, high in inside:
                d = c - b
                if d not in shifted_by:
                    parts = [(rows[pl.ds(e - d, steps, stride=16), :], 24 * e, 24 * e + 24) for e in range(GRP) if 0 <= e - d < 16]
                    shifted_by[d] = turned(merge(lane, parts), -24 * d)
                pieces.append((shifted_by[d], low, high))
            tiles[pl.ds((group * GRP + c) * 3 * steps + r, steps, stride=3), :] = merge(lane, pieces)


def load_raw(raw, tiles, count):
    pad = tiles.shape[0] // ROOM
    for n in range(count):
        tiles[pl.ds(n, SEC, stride=pad), :] = raw[:, n * LANES:(n + 1) * LANES].astype(F32)


def store_raw(tiles, raw, count):
    pad = tiles.shape[0] // ROOM
    for n in range(count):
        raw[:, n * LANES:(n + 1) * LANES] = tiles[pl.ds(n, SEC, stride=pad), :].astype(BF16)


def load_wire(wire, tiles):
    for q in range(16):
        for m in range(SEC // 2):
            pair = wire[q, 16 * m:16 * m + 16, :].astype(F32)
            at = 2 * m * TILES + 8 * q
            tiles[at:at + 8, :] = pair[:8]
            tiles[at + TILES:at + TILES + 8, :] = pair[8:]


def store_wire(tiles, wire):
    for q in range(16):
        for m in range(SEC // 2):
            at = 2 * m * TILES + 8 * q
            pair = jnp.concatenate([tiles[at:at + 8, :], tiles[at + TILES:at + TILES + 8, :]], 0)
            wire[q, 16 * m:16 * m + 16, :] = pair.astype(BF16)


def site_rows(blocks, group, rows, spread):
    flat_to_rows(blocks, group, 8, rows)
    for s in range(PHYS):
        spread[pl.ds(s, BLK, stride=PHYS), :] = rows[s * BLK:(s + 1) * BLK, :]


def diagonal(rows, s):
    lane = lane_ids(BLK)
    block = rows[s * BLK:(s + 1) * BLK, :]
    parts = [jnp.where(between(lane, 24 * c, 24 * c + 24), block, 0.0) for c in range(GRP)]
    parts.append(jnp.zeros((8, LANES), F32))
    return jnp.concatenate(parts, 0)


def widen(operator, wide, held):
    held[...] = jnp.zeros((2 * WPAD * 8, LANES), F32)
    for t in range(PHYS):
        value = operator[pl.ds(t, WPAD, stride=PHYS), :]
        for i in range(2):
            held[pl.ds(WPAD * 8 * i + PHYS * i + t, WPAD, stride=8), :] = value
    wide[...] = jnp.concatenate([held[:WD * 8, :], held[WPAD * 8:WPAD * 8 + WD * 8, :]], 1).astype(BF16)


def left_step(rows, rows_a, spread_a, operator, middle, spread):
    diag = jnp.concatenate([diagonal(rows_a, s) for s in range(PHYS)], 1).astype(BF16)
    last = spread_a[...].T.astype(BF16)
    env = jnp.concatenate([rows[pl.ds(d, WPAD, stride=BLK), :] for d in range(BLK)], 0).astype(BF16)
    xs = jnp.dot(env, diag, preferred_element_type=F32).astype(BF16)
    for p in range(6):
        x = xs[128 * p:128 * p + 128]
        for n in range(2):
            for s in range(PHYS):
                at = (4 * n + s) * WPAD
                spread[p, at:at + WPAD, :LANES] = x[n * WPAD:(n + 1) * WPAD, s * LANES:(s + 1) * LANES]
                spread[p, at:at + WPAD, LANES:] = x[64 + n * WPAD:64 + (n + 1) * WPAD, s * LANES:(s + 1) * LANES]
    for p in range(6):
        y = jnp.dot(operator[...], spread[p], preferred_element_type=F32)
        even = y[:, :LANES].reshape(WD, 8, LANES)
        odd = y[:, LANES:].reshape(WD, 8, LANES)
        middle[:, 16 * p:16 * p + 16, :] = jnp.concatenate([even, odd], 1).astype(BF16)
    lane = lane_ids(BLK)
    for u in range(WD // 2):
        y = jnp.concatenate([middle[2 * u], middle[2 * u + 1]], 1)
        out = jnp.dot(last, y, preferred_element_type=F32)
        for h in range(2):
            half = out[:, h * LANES:(h + 1) * LANES]
            acc = jnp.zeros((BLK, LANES), F32)
            for c in range(GRP):
                acc = jnp.where(between(lane, 24 * c, 24 * c + 24), half[24 * c:24 * c + 24], acc)
            rows[(2 * u + h) * BLK:(2 * u + h + 1) * BLK, :] = acc


def right_step(rows, rows_a, spread_a, operator, middle, spread):
    first = spread_a[...].astype(BF16)
    diag = jnp.concatenate([diagonal(rows_a, s).T for s in range(PHYS)], 0).astype(BF16)
    lane = lane_ids(BLK)
    zeros = jnp.zeros((8, LANES), F32)
    for u in range(WD // 2):
        halves = []
        for h in range(2):
            block = rows[(2 * u + h) * BLK:(2 * u + h + 1) * BLK, :]
            parts = [jnp.where(between(lane, 24 * c, 24 * c + 24), block, 0.0) for c in range(GRP)]
            halves.append(jnp.concatenate(parts + [zeros], 0))
        z = jnp.dot(first, jnp.concatenate(halves, 1).astype(BF16), preferred_element_type=F32)
        even = z[:, :LANES].reshape(12, 8, LANES)
        odd = z[:, LANES:].reshape(12, 8, LANES)
        middle[:, 16 * u:16 * u + 16, :] = jnp.concatenate([even, odd], 1).astype(BF16)
    for p in range(6):
        z = jnp.concatenate([middle[2 * p], middle[2 * p + 1]], 1)
        v = jnp.dot(operator[...], z, preferred_element_type=F32).astype(BF16)
        for h in range(2):
            for t in range(PHYS):
                spread[LANES * p + 64 * h:LANES * p + 64 * h + 64, t * LANES:(t + 1) * LANES] = v[64 * t:64 * t + 64, h * LANES:(h + 1) * LANES]
    out = jnp.dot(spread[...], diag, preferred_element_type=F32)
    for d in range(BLK):
        rows[pl.ds(d, WPAD, stride=BLK), :] = out[d * WPAD:(d + 1) * WPAD, :]


def load_sites(site, block):
    if site.shape[0] == SEC:
        for c in range(SEC):
            block[c * 24 + 16:c * 24 + 24, :] = jnp.zeros((8, LANES), F32)
        load_raw(site, block, 18)
    else:
        block[:SEC * 24, :] = site[...].astype(F32)


def clear_tails(tiles):
    for c in range(SEC):
        tiles[c * TILES + 120:(c + 1) * TILES, :] = jnp.zeros((TILES - 120, LANES), F32)


def load_part(part, tiles, groups):
    for m in range(GRP * groups[1]):
        at = (GRP * groups[0] + m) * TILES
        tiles[at:at + LANES, :] = part[m].astype(F32)


def store_part(tiles, part, groups):
    for m in range(GRP * groups[1]):
        at = (GRP * groups[0] + m) * TILES
        part[m] = tiles[at:at + LANES, :].astype(BF16)


def update_kernel(steps, source, result, groups, count, noted, *refs):
    env, sites, operator = refs[0], refs[1:1 + len(steps)], refs[1 + len(steps)]
    note = refs[2 + len(steps)] if noted else None
    refs = refs[count:]
    out, tiles, rows, rows_a, spread_a, middle = refs[:6]
    blocks = refs[6:6 + len(sites)]
    if steps[0] == "L":
        widen(operator, *refs[7 + len(sites):])
        operator = refs[7 + len(sites)]
    if source != "rows":
        clear_tails(tiles)
        (load_raw if source == "raw" else load_wire)(env, tiles, *([ENV // LANES] if source == "raw" else []))
    else:
        for local in range(groups[1]):
            rows[local, WD * BLK:, :] = jnp.zeros(((WPAD - WD) * BLK, LANES), F32)
    for site, block in zip(sites, blocks):
        load_sites(site, block)

    def enter(local):
        if source == "rows":
            rows.at[local][:WD * BLK, :] = env[local].astype(F32)
        else:
            flat_to_rows(tiles, local + groups[0], 48, rows.at[local])
        for n, block in enumerate(blocks):
            site_rows(block, local + groups[0], rows_a.at[local, n], spread_a.at[local, n])

    def leave(local):
        if result == "rows":
            out[local] = rows.at[local][:WD * BLK, :].astype(BF16)
        else:
            rows_to_flat(rows.at[local], local + groups[0], 48, tiles)

    enter(0)
    for local in range(groups[1]):
        if local + 1 < groups[1]:
            enter(local + 1)
        for n, step in enumerate(steps):
            (left_step if step == "L" else right_step)(
                rows.at[local], rows_a.at[local, n], spread_a.at[local, n], operator, middle.at[local % 2], refs[6 + len(sites)])
        if local > 0:
            leave(local - 1)
    leave(groups[1] - 1)
    if result == "part":
        store_part(tiles, out, groups)
    elif result == "raw":
        store_raw(tiles, out, ENV // LANES)
    elif result == "wire":
        if noted:
            tiles[pl.ds(126, SEC, stride=TILES), :] = note[...].astype(F32)
        store_wire(tiles, out)


def update(steps, source, result, groups, env, sites, operator, note=None, *tickets):
    shape = {"rows": (groups[1], WD * BLK, LANES), "part": (GRP * groups[1], LANES, LANES), "wire": (16, 160, LANES), "raw": (SEC, ENV)}[result]
    middle = (WD, 96, LANES) if steps[0] == "L" else (12, 224, LANES)
    inputs = [env, *sites, operator] + ([] if note is None else [note]) + list(tickets)
    return pl.pallas_call(
        functools.partial(update_kernel, steps, source, result, groups, len(inputs), note is not None),
        out_shape=jax.ShapeDtypeStruct(shape, BF16),
        in_specs=[pl.BlockSpec(memory_space=pltpu.VMEM)] * (len(inputs) - len(tickets)) + [pl.BlockSpec(memory_space=pl.ANY)] * len(tickets),
        out_specs=pl.BlockSpec(memory_space=pltpu.VMEM),
        scratch_shapes=[
            pltpu.VMEM((ROOM * TILES, LANES), F32),
            pltpu.VMEM((groups[1], WPAD * BLK, LANES), F32),
            pltpu.VMEM((groups[1], len(sites), LANES, LANES), F32),
            pltpu.VMEM((groups[1], len(sites), PHYS * BLK, LANES), F32),
            pltpu.VMEM((2,) + middle, BF16),
        ] + [pltpu.VMEM((ROOM * 24, LANES), F32)] * len(sites)
        + ([pltpu.VMEM((6, 256, 256), BF16), pltpu.VMEM((WD * 8, 2 * LANES), BF16), pltpu.VMEM((2 * WPAD * 8, LANES), F32)]
           if steps[0] == "L" else [pltpu.VMEM((WPAD * BLK, 4 * LANES), BF16)]),
        compiler_params=pltpu.CompilerParams(vmem_limit_bytes=16 * 1024 * 1024),
        cost_estimate=pl.CostEstimate(flops=(2000000000 if steps[0] == "L" else 50000000) * groups[1] * len(sites), bytes_accessed=100000, transcendentals=0),
        name="update_" + "".join(steps).lower() + str(groups[0]),
    )(*inputs)


def left_operator(op):
    extra = (0, WPAD - WD)
    return jnp.pad(op.transpose(1, 2, 3, 0), (extra, (0, 0), (0, 0), extra)).reshape(WPAD * PHYS, LANES).astype(F32)


def right_operator(op):
    same = jnp.eye(2, dtype=BF16)
    wide = jnp.pad(op, ((0, WPAD - WD), (0, 0), (0, 0), (0, 0)))
    return jnp.einsum("wvts,ab->tawvbs", wide, same).reshape(8 * WPAD, WD * 8)


def call(kernel, name, shapes, inputs, scratch, in_smem=0):
    spaces = [pltpu.SMEM] * in_smem + [pltpu.VMEM] * (len(inputs) - in_smem)
    return pl.pallas_call(
        kernel,
        out_shape=[jax.ShapeDtypeStruct(shape, BF16) for shape in shapes],
        in_specs=[pl.BlockSpec(memory_space=space) for space in spaces],
        out_specs=[pl.BlockSpec(memory_space=pltpu.VMEM)] * len(shapes),
        scratch_shapes=scratch,
        compiler_params=pltpu.CompilerParams(vmem_limit_bytes=16 * 1024 * 1024),
        cost_estimate=pl.CostEstimate(flops=2000000000, bytes_accessed=100000, transcendentals=0),
        name=name,
    )(*inputs)


def wire_kernel(raw, out, tiles):
    clear_tails(tiles)
    load_raw(raw, tiles, ENV // LANES)
    store_wire(tiles, out)


def to_wire(raw):
    return call(wire_kernel, "to_wire", [(16, 160, LANES)], [raw], [pltpu.VMEM((ROOM * TILES, LANES), F32)])[0]


def permute_wire(order, wire, out, held):
    for q in range(16):
        for m in range(SEC // 2):
            at = (q * SEC + 2 * m) * 8
            held[at:at + 16, :] = wire[q, 16 * m:16 * m + 16, :].astype(F32)
    for q in range(16):
        for m in range(SEC // 2):
            pair = [held[pl.ds(pl.multiple_of(order[q * SEC + 2 * m + h] * 8, 8), 8), :] for h in range(2)]
            out[q, 16 * m:16 * m + 16, :] = jnp.concatenate(pair, 0).astype(BF16)


def permute_pack_kernel(order, chosen, wire, sites, out, held, block):
    permute_wire(order, wire, out, held)
    load_sites(sites, block)
    for q in range(16):
        pair = [block[pl.ds(pl.multiple_of(chosen[2 * q + h] * 24, 8), 24), :] for h in range(2)]
        out[q, 160:208, :] = jnp.concatenate(pair, 0).astype(BF16)


def permute_pack(order, chosen, wire, sites):
    scratch = [pltpu.VMEM((16 * 160, LANES), F32), pltpu.VMEM((ROOM * 24, LANES), F32)]
    return call(permute_pack_kernel, "permute_pack", [(16, 208, LANES)], [order, chosen, wire, sites], scratch, 2)[0]


def fetch_kernel(places, wire, fetched, extra):
    for q in range(16):
        extra[q * 48:q * 48 + 48, :] = wire[q, 160:208, :].astype(F32)
    for m in range(SEC // 2):
        pair = [extra[pl.ds(pl.multiple_of(places[2 * m + h] * 24, 8), 24), :] for h in range(2)]
        fetched[48 * m:48 * m + 48, :] = jnp.concatenate(pair, 0).astype(BF16)


def fetch(places, wire):
    return call(fetch_kernel, "fetch", [(SEC * 24, LANES)], [places, wire], [pltpu.VMEM((16 * 48, LANES), F32)], 1)[0]


def touch_kernel(*refs):
    refs[-1][...] = jnp.zeros((16, LANES), BF16)


def touch(*values):
    return pl.pallas_call(
        touch_kernel,
        out_shape=jax.ShapeDtypeStruct((16, LANES), BF16),
        in_specs=[pl.BlockSpec(memory_space=pl.ANY)] * len(values),
        out_specs=pl.BlockSpec(memory_space=pltpu.VMEM),
        cost_estimate=pl.CostEstimate(flops=20000000000, bytes_accessed=1000, transcendentals=0),
        name="touch",
    )(*values)


def join_kernel(*refs):
    parts, out, tiles = refs[:-2], refs[-2], refs[-1]
    for part, groups in zip(parts, PIECES):
        load_part(part, tiles, groups)
    store_raw(tiles, out, ENV // LANES)


def join(*parts):
    return call(join_kernel, "join", [(SEC, ENV)], parts, [pltpu.VMEM((ROOM * TILES, LANES), F32)])[0]


def shifted(x, by):
    length = lax.axis_size("blk")
    return lax.ppermute(x, "blk", [(i, (i + by) % length) for i in range(length)])


def exchanged(x):
    return lax.all_to_all(x, "panel", split_axis=0, concat_axis=0, tiled=True)


def after(x, *others):
    return lax.optimization_barrier((x, *others))[0]


def pick(values, index):
    hits = index[:, None] == jnp.arange(values.shape[0])[None, :]
    return jnp.sum(jnp.where(hits, values[None, :], 0), axis=1)


def right_order(c0, s0, c1, s1):
    panels = jnp.arange(16)[:, None]
    offset, slot = c1 + pick(c0, s1), pick(s0, s1)
    return ((panels + offset[None, :]) % 16 * SEC + slot[None, :]).reshape(-1)


def left_order(c1, s1, c2, s2):
    panels = jnp.arange(16)[:, None]
    offset, slot = c2 + pick(c1, s2), pick(s1, s2)
    hits = jnp.arange(SEC)[:, None] == slot[None, :]
    source = jnp.sum(jnp.where(hits, jnp.arange(SEC)[None, :], 0), axis=1)
    back = jnp.sum(jnp.where(hits, offset[None, :], 0), axis=1)
    return ((panels - back[None, :]) % 16 * SEC + source[None, :]).reshape(-1)


def move_plan(me, c1, s1):
    slots = jnp.arange(SEC)
    rank = jnp.sum((c1[None, :] == c1[:, None]) & (slots[None, :] < slots[:, None]), axis=1)
    place = jnp.arange(32)
    same = (place % 2)[:, None] == rank[None, :]
    asked = same & (((me - place // 2) % 16)[:, None] == c1[None, :])
    pushed = same & (((place // 2 - me) % 16)[:, None] == c1[None, :])
    chosen = [jnp.sum(jnp.where(asked, s1[None, :], 0), axis=1), jnp.sum(jnp.where(pushed, slots[None, :], 0), axis=1)]
    landing = slots[:, None] == s1[None, :]
    back = jnp.sum(jnp.where(landing, ((me - c1) % 16 * 2 + rank)[None, :], 0), axis=1)
    return chosen, [(me + c1) % 16 * 2 + rank, back]


def masked(tensor, rows, cols, noted):
    place = jnp.arange(tensor.shape[1] + LANES)
    live = place < tensor.shape[1]
    keep = live & ((place // BLK % BLK)[None, :] < rows[:, None]) & ((place % BLK)[None, :] < cols[:, None])
    tensor = jnp.pad(tensor, ((0, 0), (0, LANES)))
    extra = jnp.where(place == SITE, (noted // SEC)[:, None], jnp.where(place == SITE + 1, (noted % SEC)[:, None], 0))
    return jnp.where(keep, tensor, extra.astype(BF16))


def body(left_env, right_env, site_tensors, chain_operator, targets, sector_dims):
    me = lax.axis_index("panel")
    wire = to_wire(right_env[0])
    arrived = exchanged(wire)

    target = targets[0]
    code = (target // SEC - me) % 16 * SEC + target % SEC
    rows = lax.dynamic_slice_in_dim(sector_dims, me * SEC, SEC)
    blocks = after(masked(site_tensors[0], rows, pick(sector_dims, target), code), wire)
    blocks1 = shifted(blocks, 1)
    operator = left_operator(after(chain_operator, wire))
    left = update(("L",), "raw", "wire", WHOLE, left_env[0], [blocks], operator, blocks[:, SITE:])
    left_moved = shifted(left, 2)

    noted = blocks1[:, SITE:SITE + 2].astype(jnp.int32)
    c0, s0, c1, s1 = code // SEC, code % SEC, noted[:, 0], noted[:, 1]
    chosen, places = move_plan(me, c1, s1)
    wire = permute_pack(right_order(c0, s0, c1, s1), chosen[0], after(arrived, left), blocks)
    right = exchanged(wire)
    fetched = fetch(places[0], right)

    operator_r = right_operator(after(chain_operator, wire))
    left = exchanged(after(left_moved, fetched))
    def right_piece(number, *order):
        tickets = [touch(left_moved)] if number == 0 else []
        piece = update(("R", "R"), "wire", "part", PIECES[number], after(right, *order), [fetched, blocks1], operator_r, None, *tickets)
        return piece, shifted(piece, -2)

    right0, moved0 = right_piece(0)
    noted = after(left_moved, right0)[15].reshape(SEC, 8, LANES)[:, 6, :2].astype(jnp.int32)
    ordered = permute_pack(left_order(c1, s1, noted[:, 0], noted[:, 1]), chosen[1], left, blocks1)
    left = exchanged(ordered)
    right1, moved1 = right_piece(1, right0, ordered)
    left_out = update(("L",), "wire", "raw", WHOLE, left, [fetch(places[1], left)], operator, None, touch(after(moved0, right1)))
    right_out = join(after(moved0, left_out), moved1)
    return left_out[None], right_out[None]


def solution(mesh):
    whole = P("blk", "panel", None)
    return jax.shard_map(
        body,
        mesh=mesh,
        in_specs=(whole, whole, whole, P(), P("blk", "panel"), P()),
        out_specs=(whole, whole),
        check_vma=False,
    )
```
